256 devices in a mesh: patch: 32 (over y, z), visit: 8 (over x, core).
Axes of the slice: x: 4, y: 4, z: 8, core: 2. Of those that a mesh axis runs over, the one named last changes fastest.
Arguments:
- blocks: bfloat16 [8, 2048, 128, 128], P('visit', 'patch'), may hold values from -6 to 6
- send_list: int32 [8, 32, 2, 16], P('visit', 'patch'), may hold values from -1 to 63, as said below
- block_slot: int32 [8, 2048], P('visit', 'patch'), may hold values from 0 to 63, as said below
- block_offset: int32 [8, 2048, 2], P('visit', 'patch'), may hold values from -2 to 2
- block_frac: bfloat16 [8, 2048, 2], P('visit', 'patch'), may hold values from 0.049804688 to 0.94921875
- inv_var: bfloat16 [8, 2048], P('visit', 'patch'), may hold values from 0.29882812 to 3
- psf_kernel: float32 [8, 25, 25], P('visit'), may hold values from -0.24 to 0.24
Outputs:
- coadded: float32 [32768, 1024], P('patch', 'visit')
The draws below stay inside these ranges and needn't reach their ends.
Inputs may be any that keep to these rules, and one draw needn't show every extreme that they name: `send_list`: each device's two lists hold distinct local blocks; device 0's list toward a lower patch and the last device's list toward a higher patch are all -1, every other list is full. `block_slot`: every slot of every patch receives exactly one block of every visit.
All inputs are finite; a program needn't handle non-finite values.
Results may differ from the reference program's by a relative error of at most 0.0066.
Values may be sent and summed in bfloat16 or wider, within the bound.
A program may use at most 64 MiB of HBM per device.

```python
import math
import jax
import jax.numpy as jnp
from jax import lax

BLOCK = 128
SLOT_ROWS = 8
SLOT_COLS = 8
SLOTS = 64
KSIZE = 25
BLK_DEV = 64
CAP = 16
VISITS = 8
TRACT_ROWS = 32768
WIDTH = 1024
N_PATCH = 32


def footprint(key):

    def shuffle_one(row_key):
        return jax.random.permutation(row_key, BLK_DEV).astype(jnp.int32)

    def one_visit(visit_key):
        key_order, key_local = jax.random.split(visit_key, 2)
        slot_order = jax.random.permutation(key_order, SLOTS).astype(jnp.int32)
        local_ids = jax.vmap(shuffle_one)(jax.random.split(key_local, N_PATCH))
        device_ids = jnp.arange(N_PATCH).astype(jnp.int32)[:, None]
        lower_ids = local_ids[:, 2 * CAP:3 * CAP]
        upper_ids = local_ids[:, 3 * CAP:]
        list_lower = jnp.where(device_ids > 0, lower_ids, -1)
        list_upper = jnp.where(device_ids < N_PATCH - 1, upper_ids, -1)
        list_table = jnp.stack([list_lower, list_upper], axis=1)
        position = jnp.broadcast_to(jnp.arange(BLK_DEV).astype(jnp.int32)[None, :], (N_PATCH, BLK_DEV))
        goes_lower = (position >= 2 * CAP) & (position < 3 * CAP) & (device_ids > 0)
        goes_upper = (position >= 3 * CAP) & (device_ids < N_PATCH - 1)
        order_index = jnp.where(goes_lower, position + CAP, jnp.where(goes_upper, position - CAP, position))
        slot_values = slot_order[order_index]
        row_ids = jnp.broadcast_to(device_ids, (N_PATCH, BLK_DEV))
        slot_table = jnp.zeros((N_PATCH, BLK_DEV), jnp.int32).at[row_ids, local_ids].set(slot_values)
        return (list_table.astype(jnp.int32), slot_table.reshape(-1))
    return jax.vmap(one_visit)(jax.random.split(key, VISITS))


def draw_send_list(key, part):
    return footprint(jax.random.fold_in(key, 7))[0].astype(jnp.int32)


def draw_block_slot(key, part):
    return footprint(jax.random.fold_in(key, 7))[1].astype(jnp.int32)


def set_ends(result, rng, least, high):
    longest = result.shape.index(max(result.shape))
    spots = []
    for shift in (0, 1):
        where = [jax.random.randint(jax.random.fold_in(rng, axis), (), 0, length) for axis, length in enumerate(result.shape)]
        where[longest] = (where[longest] + shift) % result.shape[longest]
        spots.append(tuple(where))
    return result.at[spots[0]].set(least).at[spots[1]].set(high)


def level_of(key, shape, cuts, least, largest):
    def one(dim, parts):
        heights = jax.random.uniform(jax.random.fold_in(jax.random.fold_in(key, 6), dim), (parts,), jnp.float32, least / len(cuts), largest / len(cuts))
        return jnp.repeat(jnp.exp(heights), shape[dim] // parts).reshape((-1,) + (1,) * (len(shape) - dim - 1))

    factor_of = one(*cuts[0])
    for cut in cuts[1:]:
        factor_of = factor_of * one(*cut)
    return factor_of


def noise(key, extent, width, most, pieces=(), kind=jnp.bfloat16):
    values = width * jax.random.normal(key, extent, jnp.float32)
    if pieces:
        values = values * level_of(key, extent, pieces, -0.22, 0.18)
    return jnp.clip(values, -most, most).astype(kind)


def setup_inputs(seed: int = 0) -> dict:
    streams_of = jax.random.split(jax.random.key(seed), 8)
    return {
        "blocks": noise(streams_of[0], (VISITS, N_PATCH * BLK_DEV, BLOCK, BLOCK), 1.0, 6.0, ((0, 8), (1, 32))),
        "send_list": draw_send_list(jax.random.fold_in(streams_of[7], 71), 0),
        "block_slot": draw_block_slot(jax.random.fold_in(streams_of[7], 71), 0),
        "block_offset": set_ends(jax.random.randint(streams_of[3], (VISITS, N_PATCH * BLK_DEV, 2), -2, 3), jax.random.fold_in(streams_of[3], 1), -2, 2).astype(jnp.int32),
        "block_frac": jnp.clip(0.049804688 + 0.89941406 * jax.random.uniform(streams_of[4], (VISITS, N_PATCH * BLK_DEV, 2), jnp.float32) ** level_of(streams_of[4], (VISITS, N_PATCH * BLK_DEV, 2), ((0, 8), (1, 32)), -0.2, 0.2), 0.049804688, 0.94921875).astype(jnp.bfloat16),
        "inv_var": jnp.clip(jnp.exp(math.log(3.0) - 2.306499 * jax.random.uniform(streams_of[5], (VISITS, N_PATCH * BLK_DEV), jnp.float32) ** level_of(streams_of[5], (VISITS, N_PATCH * BLK_DEV), ((0, 8), (1, 32)), -0.2, 0.2)), 0.29882812, 3.0).astype(jnp.bfloat16),
        "psf_kernel": noise(streams_of[6], (VISITS, KSIZE, KSIZE), 0.04, 0.24, ((0, 8),), jnp.float32),
    }


def lanczos_weight(tap_offset):
    inside = jnp.abs(tap_offset) < 3.0
    safe_tap = jnp.where(inside, tap_offset, 1.5)
    value = 3.0 * jnp.sin(math.pi * safe_tap) * jnp.sin(math.pi * safe_tap / 3.0) / (math.pi * math.pi * safe_tap * safe_tap)
    return jnp.where(inside, value, 0.0)


def lanczos_matrix(shift, edge_len):
    positions = jnp.arange(edge_len).astype(shift.dtype)
    tap_offset = positions[None, None, :] - positions[None, :, None] - shift[:, None, None]
    return lanczos_weight(tap_offset).astype(jnp.bfloat16)


def warp_blocks(pixels, row_shift, col_shift):
    edge_len = pixels.shape[-1]
    row_mat = lanczos_matrix(row_shift, edge_len)
    col_mat = lanczos_matrix(col_shift, edge_len)
    first = jnp.einsum('nim,nmk->nik', row_mat.astype(jnp.float32), pixels.astype(jnp.float32)).astype(jnp.bfloat16)
    return jnp.einsum('nik,njk->nij', first.astype(jnp.float32), col_mat.astype(jnp.float32)).astype(jnp.bfloat16)


def reference(blocks, send_list, block_slot, block_offset, block_frac, inv_var, psf_kernel):
    half_reach = KSIZE // 2
    numer = jnp.zeros((TRACT_ROWS, WIDTH), jnp.float32)
    denom = jnp.zeros((N_PATCH * SLOT_ROWS, WIDTH), jnp.float32)
    patch_ids = jnp.arange(N_PATCH).astype(jnp.int32)
    for visit_id in range(VISITS):
        shifts = block_offset[visit_id].astype(jnp.float32) + block_frac[visit_id].astype(jnp.float32)
        warped = warp_blocks(blocks[visit_id], shifts[:, 0], shifts[:, 1])
        list_table = send_list[visit_id]
        source_ids = patch_ids[:, None, None] * BLK_DEV + list_table
        source_ids = jnp.where(list_table >= 0, source_ids, N_PATCH * BLK_DEV).astype(jnp.int32)
        target_ids = patch_ids[:, None, None] - 1 + 2 * jnp.arange(2).astype(jnp.int32)[None, :, None]
        target_ids = jnp.broadcast_to(target_ids, list_table.shape).astype(jnp.int32)
        home_patch = jnp.concatenate([jnp.repeat(patch_ids, BLK_DEV), jnp.zeros((1,), jnp.int32)])
        dest_patch = home_patch.at[source_ids.reshape(-1)].set(target_ids.reshape(-1))[:-1]
        global_slot = (dest_patch * SLOTS + block_slot[visit_id]).astype(jnp.int32)
        weights = inv_var[visit_id].astype(jnp.float32)
        slot_sum = jax.ops.segment_sum(weights[:, None, None] * warped.astype(jnp.float32), global_slot, num_segments=N_PATCH * SLOTS)
        visit_image = slot_sum.reshape(N_PATCH, SLOT_ROWS, SLOT_COLS, BLOCK, BLOCK).transpose(0, 1, 3, 2, 4).reshape(TRACT_ROWS, WIDTH).astype(jnp.bfloat16)
        slot_weight = jax.ops.segment_sum(weights, global_slot, num_segments=N_PATCH * SLOTS).reshape(N_PATCH * SLOT_ROWS, SLOT_COLS)
        denom = denom + jnp.repeat(slot_weight, BLOCK, axis=1)
        kernel = psf_kernel[visit_id].astype(jnp.bfloat16).astype(jnp.float32)
        blurred = lax.conv_general_dilated(visit_image.astype(jnp.float32)[None, None], kernel[None, None], (1, 1), ((half_reach, half_reach), (half_reach, half_reach)), precision=lax.Precision.HIGHEST)
        numer = numer + blurred[0, 0]
    return numer / jnp.repeat(denom, BLOCK, axis=0)
```

```python
import math

import jax
import jax.numpy as jnp
from jax import lax
from jax.experimental import pallas as pl
from jax.experimental.pallas import tpu as pltpu
from jax.sharding import PartitionSpec as P

EDGE = 128
BLOCKS = 64
CAP = 16
KSIZE = 25
REACH = 12
GROUP = 8
SLOT_COLS = 8
SLOT_ROWS = 8
ROWS = SLOT_ROWS * EDGE
COLS = SLOT_COLS * EDGE
HALO = 16
EXT_ROWS = ROWS + 2 * HALO
SEGS = 16
SEG_ROWS = ROWS // SEGS
PAIRS = SEG_ROWS // 2
STEPS = KSIZE // 2 + 1
EXT_PAIRS = PAIRS + STEPS - 1
OUT_WIN = EDGE - 2 * REACH
WINDOWS = -(-COLS // OUT_WIN)
F32 = jnp.float32
BF16 = jnp.bfloat16


def lanczos_weight(tap_offset):
    inside = jnp.abs(tap_offset) < 3.0
    safe_tap = jnp.where(inside, tap_offset, 1.5)
    value = (
        3.0
        * jnp.sin(math.pi * safe_tap)
        * jnp.sin(math.pi * safe_tap / 3.0)
        / (math.pi * math.pi * safe_tap * safe_tap)
    )
    return jnp.where(inside, value, 0.0)


def column_of(row):
    count = row.shape[1]
    down = lax.broadcasted_iota(jnp.int32, (count, count), 0)
    across = lax.broadcasted_iota(jnp.int32, (count, count), 1)
    spread = jnp.where(down == across, jnp.broadcast_to(row, (count, count)), 0.0)
    return jnp.sum(spread, axis=1, keepdims=True)


def warp_kernel(
    list_ref,
    slot_ref,
    list_vec,
    slot_vec,
    offset_ref,
    frac_ref,
    weight_ref,
    blocks_ref,
    own_ref,
    index_ref,
    slot_weight_ref,
    row_taps,
    col_taps,
    weights,
    place,
):
    step = pl.program_id(0)
    patch = lax.axis_index("patch")
    last = lax.axis_size("patch") - 1

    @pl.when(step == 0)
    def prepare():
        shift = offset_ref[...].astype(F32) + frac_ref[...].astype(F32)
        lane = lax.broadcasted_iota(jnp.int32, (BLOCKS, EDGE), 1)
        signed = jnp.where(lane < EDGE // 2, lane, lane - EDGE).astype(F32)
        row_taps[...] = lanczos_weight(signed - shift[:, 0:1]).astype(BF16).astype(F32)
        col_taps[...] = lanczos_weight(-signed - shift[:, 1:2]).astype(BF16).astype(F32)
        weight = column_of(weight_ref[...].astype(F32))
        weights[...] = jnp.broadcast_to(weight, (BLOCKS, EDGE))

        ids = lax.broadcasted_iota(jnp.int32, (BLOCKS, CAP), 0)
        low = jnp.sum(jnp.where(list_vec[0:1, :] == ids, 1.0, 0.0), axis=1, keepdims=True)
        high = jnp.sum(jnp.where(list_vec[1:2, :] == ids, 1.0, 0.0), axis=1, keepdims=True)
        slot = column_of(slot_vec[...].astype(F32))
        spread = jnp.where(slot == lane.astype(F32), weight, 0.0)
        slot_weight_ref[...] = jnp.zeros_like(slot_weight_ref)
        slot_weight_ref[0:1, :] = jnp.sum(spread * (1.0 - low - high), axis=0, keepdims=True)
        slot_weight_ref[1:2, :] = jnp.sum(spread * low, axis=0, keepdims=True)
        slot_weight_ref[2:3, :] = jnp.sum(spread * high, axis=0, keepdims=True)

        def clear(j, carry):
            place[j] = -1
            for k in range(3):
                index_ref[k, j] = 0
            return carry

        lax.fori_loop(0, BLOCKS, clear, 0)

        def mark(t, carry):
            for side in range(2):
                j = list_ref[side, t]

                @pl.when(j >= 0)
                def leaves():
                    place[j] = side * CAP + t
                    index_ref[1 + side, slot_ref[0, j]] = (5 - side) * CAP + t + 1

            return carry

        lax.fori_loop(0, CAP, mark, 0)

        def fill(j, free):
            stays = place[j] < 0

            @pl.when(stays)
            def keep():
                place[j] = free
                index_ref[0, slot_ref[0, j]] = free + 1

            after = free + stays.astype(jnp.int32)
            return jnp.where((patch == 0) & (after == CAP), 2 * CAP, after)

        first_free = jnp.where(patch == 0, 0, jnp.where(patch == last, CAP, 2 * CAP))
        lax.fori_loop(0, BLOCKS, fill, first_free)

    down = lax.broadcasted_iota(jnp.int32, (EDGE, EDGE), 0)
    across = lax.broadcasted_iota(jnp.int32, (EDGE, EDGE), 1)
    near = jnp.abs(down - across) < EDGE // 2

    def band(taps_ref, j):
        taps = jnp.broadcast_to(taps_ref[pl.ds(j, 1), :], (EDGE, EDGE))
        rolled = pltpu.roll(taps, 0, 1, stride=1, stride_axis=0)
        return jnp.where(near, rolled, 0.0).astype(BF16)

    for local in range(GROUP):
        j = step * GROUP + local
        first = jnp.dot(band(row_taps, j), blocks_ref[local], preferred_element_type=F32)
        warped = jnp.dot(first.astype(BF16), band(col_taps, j), preferred_element_type=F32)
        scaled = warped.astype(BF16).astype(F32) * weights[pl.ds(j, 1), :]
        own_ref[place[j]] = scaled.astype(BF16)


def whole(shape, space=pltpu.VMEM):
    zeros = (0,) * len(shape)
    return pl.BlockSpec(shape, lambda *_: zeros, memory_space=space)


def warp(blocks, send_list, block_slot, block_offset, block_frac, inv_var):
    return pl.pallas_call(
        warp_kernel,
        grid=(BLOCKS // GROUP,),
        out_shape=(
            jax.ShapeDtypeStruct((BLOCKS, EDGE, EDGE), BF16),
            jax.ShapeDtypeStruct((8, EDGE), jnp.int32),
            jax.ShapeDtypeStruct((8, EDGE), F32),
        ),
        in_specs=[
            whole((2, CAP), pltpu.SMEM),
            whole((1, BLOCKS), pltpu.SMEM),
            whole((2, CAP)),
            whole((1, BLOCKS)),
            whole((BLOCKS, 2)),
            whole((BLOCKS, 2)),
            whole((1, BLOCKS)),
            pl.BlockSpec((GROUP, EDGE, EDGE), lambda g: (g, 0, 0)),
        ],
        out_specs=(
            whole((BLOCKS, EDGE, EDGE)),
            whole((8, EDGE), pltpu.SMEM),
            whole((8, EDGE)),
        ),
        scratch_shapes=[
            pltpu.VMEM((BLOCKS, EDGE), F32),
            pltpu.VMEM((BLOCKS, EDGE), F32),
            pltpu.VMEM((BLOCKS, EDGE), F32),
            pltpu.SMEM((BLOCKS,), jnp.int32),
        ],
        compiler_params=pltpu.CompilerParams(vmem_limit_bytes=32 << 20),
        name="warp",
    )(
        send_list,
        block_slot,
        send_list,
        block_slot,
        block_offset,
        block_frac,
        inv_var,
        blocks,
    )


def remote(src, dst, send_sem, recv_sem, **target):
    return pltpu.make_async_remote_copy(
        src_ref=src,
        dst_ref=dst,
        send_sem=send_sem,
        recv_sem=recv_sem,
        device_id=target,
        device_id_type=pl.DeviceIdType.MESH,
    )


def route_kernel(
    own_ref,
    index_ref,
    weight_ref,
    image_ref,
    weight_sum_ref,
    held,
    index_in,
    weight_in,
    index_sum,
    index_flat,
    halo_in,
    send_sem,
    recv_sem,
    local_sem,
):
    me = lax.axis_index("patch")
    last = lax.axis_size("patch") - 1
    has_low, has_high = me > 0, me < last
    low, high = jnp.maximum(me - 1, 0), jnp.minimum(me + 1, last)
    sides = ((has_low, low), (has_high, high))

    barrier = pltpu.get_barrier_semaphore()
    for there, neighbour in sides:

        @pl.when(there)
        def greet():
            pl.semaphore_signal(
                barrier, inc=1, device_id={"patch": neighbour}, device_id_type=pl.DeviceIdType.MESH
            )

    pl.semaphore_wait(barrier, has_low.astype(jnp.int32) + has_high.astype(jnp.int32))

    def copy_of(kind, side, neighbour):
        lands = 1 - side
        pair = (
            (index_ref, index_in.at[lands]),
            (weight_ref, weight_in.at[lands]),
            (own_ref.at[pl.ds(side * CAP, CAP)], held.at[pl.ds((4 + lands) * CAP, CAP)]),
        )[kind]
        return remote(*pair, send_sem.at[side, kind], recv_sem.at[lands, kind], patch=neighbour)

    def halo_copy(side, neighbour):
        lands = 1 - side
        first = HALO if side == 0 else ROWS
        return remote(
            image_ref.at[:, pl.ds(first, HALO)],
            halo_in.at[lands],
            send_sem.at[side, 3],
            recv_sem.at[lands, 3],
            patch=neighbour,
        )

    for side, (there, neighbour) in enumerate(sides):

        @pl.when(there)
        def send():
            for kind in range(3):
                copy_of(kind, side, neighbour).start()

    stay = pltpu.make_async_copy(own_ref, held.at[pl.ds(0, BLOCKS)], local_sem.at[0])
    stay.start()

    for side, (there, neighbour) in enumerate(sides):

        @pl.when(jnp.logical_not(there))
        def nothing():
            index_in[side] = jnp.zeros((8, EDGE), jnp.int32)
            weight_in[side] = jnp.zeros((8, EDGE), F32)
            halo_in[side] = jnp.zeros((SLOT_COLS, HALO, EDGE), BF16)

    for side, (there, neighbour) in enumerate(sides):

        @pl.when(there)
        def arrive():
            for kind in range(2):
                copy_of(kind, 1 - side, neighbour).wait_recv()

    index_sum[...] = jnp.zeros((8, EDGE), jnp.int32)
    found = index_ref[0:1, :] + index_in[0, 2:3, :] + index_in[1, 1:2, :]
    index_sum[0:1, :] = jnp.maximum(found, 1) - 1
    weight_sum_ref[...] = jnp.zeros((8, EDGE), F32)
    weight_sum_ref[0:1, :] = weight_ref[0:1, :] + weight_in[0, 2:3, :] + weight_in[1, 1:2, :]
    flat = pltpu.make_async_copy(index_sum, index_flat, local_sem.at[1])
    flat.start()
    flat.wait()
    stay.wait()
    for side, (there, neighbour) in enumerate(sides):

        @pl.when(there)
        def arrive_blocks():
            copy_of(2, 1 - side, neighbour).wait_recv()

    def put(slot_row, carry):
        for slot_col in range(SLOT_COLS):
            source = index_flat[0, slot_row * SLOT_COLS + slot_col]
            top = pl.multiple_of(HALO + slot_row * EDGE, HALO)
            image_ref[slot_col, pl.ds(top, EDGE), :] = held[source]
        return carry

    lax.fori_loop(0, SLOT_ROWS, put, 0)

    for side, (there, neighbour) in enumerate(sides):

        @pl.when(there)
        def send_halo():
            halo_copy(side, neighbour).start()

    for side, (there, neighbour) in enumerate(sides):

        @pl.when(there)
        def arrive_halo():
            halo_copy(1 - side, neighbour).wait_recv()

    image_ref[:, 0:HALO, :] = halo_in[0]
    image_ref[:, HALO + ROWS : EXT_ROWS, :] = halo_in[1]

    for side, (there, neighbour) in enumerate(sides):

        @pl.when(there)
        def sent():
            for kind in range(3):
                copy_of(kind, side, neighbour).wait_send()
            halo_copy(side, neighbour).wait_send()


def route(own, index, slot_weight):
    vmem = pl.BlockSpec(memory_space=pltpu.VMEM)
    return pl.pallas_call(
        route_kernel,
        out_shape=(
            jax.ShapeDtypeStruct((SLOT_COLS, EXT_ROWS, EDGE), BF16),
            jax.ShapeDtypeStruct((8, EDGE), F32),
        ),
        in_specs=[pl.BlockSpec(memory_space=pl.ANY), vmem, vmem],
        out_specs=(vmem, vmem),
        scratch_shapes=[
            pltpu.VMEM((6 * CAP, EDGE, EDGE), BF16),
            pltpu.VMEM((2, 8, EDGE), jnp.int32),
            pltpu.VMEM((2, 8, EDGE), F32),
            pltpu.VMEM((8, EDGE), jnp.int32),
            pltpu.SMEM((8, EDGE), jnp.int32),
            pltpu.VMEM((2, SLOT_COLS, HALO, EDGE), BF16),
            pltpu.SemaphoreType.DMA((2, 4)),
            pltpu.SemaphoreType.DMA((2, 4)),
            pltpu.SemaphoreType.DMA((2,)),
        ],
        compiler_params=pltpu.CompilerParams(
            collective_id=0, has_side_effects=True, vmem_limit_bytes=32 << 20
        ),
        name="route",
    )(own, index, slot_weight)


def pieces_of(tile):
    found, column = [], tile * EDGE
    while column < (tile + 1) * EDGE:
        window, lane = divmod(column, OUT_WIN)
        count = min(OUT_WIN - lane, (tile + 1) * EDGE - column)
        found.append((window, lane, column - tile * EDGE, count))
        column += count
    return found


def blur_kernel(image_ref, psf_ref, part_ref, wide, windows, taps, acc):
    lane = lax.broadcasted_iota(jnp.int32, (SEGS, EDGE), 1)
    source = lax.broadcasted_iota(jnp.int32, (KSIZE, EDGE), 0)
    target = lax.broadcasted_iota(jnp.int32, (KSIZE, EDGE), 1)
    flip = jnp.where((target + source) % EDGE == 0, 1.0, 0.0).astype(BF16)
    flipped = jnp.dot(psf_ref[...].astype(BF16), flip, preferred_element_type=F32)
    for t in range(STEPS):
        for row_in in range(2):
            for row_out in range(2):
                tap_row = 2 * t + row_in - row_out
                here = (
                    slice(t * 256 + row_in * EDGE, t * 256 + (row_in + 1) * EDGE),
                    slice(row_out * EDGE, (row_out + 1) * EDGE),
                )
                if 0 <= tap_row < KSIZE:
                    spread = jnp.broadcast_to(flipped[tap_row : tap_row + 1, :], (EDGE, EDGE))
                    taps[here] = pltpu.roll(spread, 0, 1, stride=1, stride_axis=0).astype(BF16)
                else:
                    taps[here] = jnp.zeros((EDGE, EDGE), BF16)

    def widen(r, carry):
        rows = pl.ds(pl.multiple_of(r * 32, 32), 32)
        wide[:, rows, :] = image_ref[:, rows, :].astype(F32)
        return carry

    lax.fori_loop(0, EXT_ROWS // 32, widen, 0)

    nothing = jnp.zeros((SEGS, EDGE), F32)

    def spread_rows(g, carry):
        for row_in in range(2):
            start = 2 * g + (HALO - REACH) + row_in
            tiles = [
                wide[i, pl.ds(start, SEGS, stride=SEG_ROWS), :]
                for i in range(SLOT_COLS)
            ]
            for j in range(WINDOWS):
                tile, off = divmod(OUT_WIN * j - REACH, EDGE)
                left = tiles[tile] if tile >= 0 else nothing
                right = tiles[tile + 1] if tile + 1 < SLOT_COLS else nothing
                if off:
                    left = pltpu.roll(left, EDGE - off, 1) if tile >= 0 else nothing
                    right = pltpu.roll(right, EDGE - off, 1) if tile + 1 < SLOT_COLS else nothing
                    left = jnp.where(lane < EDGE - off, left, right)
                windows[j, g, :, row_in * EDGE : (row_in + 1) * EDGE] = left.astype(BF16)
        return carry

    lax.fori_loop(0, EXT_PAIRS, spread_rows, 0)

    def one_window(j, carry):
        lhs = jnp.concatenate(
            [windows[j, t : t + PAIRS].reshape(PAIRS * SEGS, 256) for t in range(STEPS)], axis=1
        )
        acc[j] = jnp.dot(lhs, taps[...], preferred_element_type=F32)
        return carry

    lax.fori_loop(0, WINDOWS, one_window, 0)

    across = lax.broadcasted_iota(jnp.int32, (SEGS, EDGE), 1)

    def gather_tiles(g, carry):
        rows = pl.ds(pl.multiple_of(g * SEGS, SEGS), SEGS)
        for row_out in range(2):
            lanes = slice(row_out * EDGE, (row_out + 1) * EDGE)
            for tile in range(SLOT_COLS):
                total = None
                for window, there, here, count in pieces_of(tile):
                    value = acc[window, rows, lanes]
                    if here != there:
                        value = pltpu.roll(value, (here - there) % EDGE, 1)
                    total = value if total is None else jnp.where(across >= here, value, total)
                part_ref[tile, pl.ds(pl.multiple_of(row_out * (ROWS // 2) + g * SEGS, SEGS), SEGS), :] = (
                    total.astype(BF16)
                )
        return carry

    lax.fori_loop(0, PAIRS, gather_tiles, 0)


def blur(image, psf):
    vmem = pl.BlockSpec(memory_space=pltpu.VMEM)
    return pl.pallas_call(
        blur_kernel,
        out_shape=jax.ShapeDtypeStruct((SLOT_COLS, ROWS, EDGE), BF16),
        in_specs=[vmem, vmem],
        out_specs=vmem,
        scratch_shapes=[
            pltpu.VMEM((SLOT_COLS, EXT_ROWS, EDGE), F32),
            pltpu.VMEM((WINDOWS, EXT_PAIRS, SEGS, 256), BF16),
            pltpu.VMEM((STEPS * 256, 256), BF16),
            pltpu.VMEM((WINDOWS, PAIRS * SEGS, 256), F32),
        ],
        compiler_params=pltpu.CompilerParams(vmem_limit_bytes=48 << 20),
        name="blur",
    )(image, psf)


def reduce_kernel(
    part_ref,
    weight_ref,
    out_ref,
    pair_in,
    pair_sum,
    chip_in,
    weight_in,
    pair_send,
    pair_recv,
    chip_send,
    chip_recv,
    weight_send,
    weight_recv,
):
    me = lax.axis_index("visit")
    count = lax.axis_size("visit")
    chips = count // 2
    chip, core = me // 2, lax.rem(me, 2)
    partner = me + 1 - 2 * core

    barrier = pltpu.get_barrier_semaphore()
    for d in range(1, count):
        pl.semaphore_signal(
            barrier, inc=1, device_id={"visit": lax.rem(me + d, count)}, device_id_type=pl.DeviceIdType.MESH
        )
    pl.semaphore_wait(barrier, count - 1)

    def pair_copy(d):
        other = lax.rem(chip + d, chips)
        return remote(
            part_ref.at[2 * other + 1 - core], pair_in.at[d], pair_send.at[d], pair_recv.at[d], visit=partner
        )

    def chip_copy(d):
        other = lax.rem(chip + d, chips)
        return remote(
            pair_sum.at[d - 1],
            chip_in.at[d - 1],
            chip_send.at[d - 1],
            chip_recv.at[d - 1],
            visit=2 * other + core,
        )

    def weight_copy(d):
        return remote(
            weight_ref,
            weight_in.at[d - 1],
            weight_send.at[d - 1],
            weight_recv.at[d - 1],
            visit=lax.rem(me + d, count),
        )

    order = [2, 1, 3, 0]
    for d in order:
        pair_copy(d).start()
    for d in range(1, count):
        weight_copy(d).start()

    for d in order[:-1]:
        other = lax.rem(chip + d, chips)
        pair_copy(d).wait_recv()

        def add(r, carry):
            rows = pl.ds(pl.multiple_of(r * 128, 128), 128)
            total = part_ref[2 * other + core, rows, :].astype(F32) + pair_in[d, rows, :].astype(F32)
            pair_sum[d - 1, rows, :] = total.astype(BF16)
            return carry

        lax.fori_loop(0, ROWS // 128, add, 0)
        chip_copy(d).start()

    for d in range(1, count):
        weight_copy(d).wait_recv()
    denom = weight_ref[0:1, :]
    for d in range(1, count):
        denom = denom + weight_in[d - 1, 0:1, :]
    lane = lax.broadcasted_iota(jnp.int32, (SEGS, EDGE), 1)
    row = lax.broadcasted_iota(jnp.int32, (SEGS, EDGE), 0)
    wanted = (row // 2) * SLOT_COLS + me
    denom = jnp.sum(jnp.where(lane == wanted, jnp.broadcast_to(denom, (SEGS, EDGE)), 0.0), axis=1, keepdims=True)
    denom = jnp.broadcast_to(denom, (SEGS, EDGE))

    pair_copy(0).wait_recv()
    for d in (1, 3, 2):
        chip_copy(d).wait_recv()

    def finish(g, carry):
        for row_out in range(2):
            rows = pl.ds(pl.multiple_of(row_out * (ROWS // 2) + g * SEGS, SEGS), SEGS)
            total = part_ref[me, rows, :].astype(F32) + pair_in[0, rows, :].astype(F32)
            for d in range(1, chips):
                total = total + chip_in[d - 1, rows, :].astype(F32)
            out_ref[pl.ds(2 * g + row_out, SEGS, stride=SEG_ROWS), :] = total / denom
        return carry

    lax.fori_loop(0, PAIRS, finish, 0)

    for d in order:
        pair_copy(d).wait_send()
    for d in range(1, chips):
        chip_copy(d).wait_send()
    for d in range(1, count):
        weight_copy(d).wait_send()


def reduce(part, weight_sum):
    vmem = pl.BlockSpec(memory_space=pltpu.VMEM)
    count = lax.axis_size("visit")
    chips = count // 2
    return pl.pallas_call(
        reduce_kernel,
        out_shape=jax.ShapeDtypeStruct((ROWS, EDGE), F32),
        in_specs=[vmem, vmem],
        out_specs=vmem,
        scratch_shapes=[
            pltpu.VMEM((chips, ROWS, EDGE), BF16),
            pltpu.VMEM((chips - 1, ROWS, EDGE), BF16),
            pltpu.VMEM((chips - 1, ROWS, EDGE), BF16),
            pltpu.VMEM((count - 1, 8, EDGE), F32),
            pltpu.SemaphoreType.DMA((chips,)),
            pltpu.SemaphoreType.DMA((chips,)),
            pltpu.SemaphoreType.DMA((chips - 1,)),
            pltpu.SemaphoreType.DMA((chips - 1,)),
            pltpu.SemaphoreType.DMA((count - 1,)),
            pltpu.SemaphoreType.DMA((count - 1,)),
        ],
        compiler_params=pltpu.CompilerParams(
            collective_id=1, has_side_effects=True, vmem_limit_bytes=32 << 20
        ),
        name="reduce",
    )(part, weight_sum)


def on_device(blocks, send_list, block_slot, block_offset, block_frac, inv_var, psf_kernel):
    own, index, slot_weight = warp(
        blocks[0], send_list[0, 0], block_slot, block_offset[0], block_frac[0], inv_var
    )
    image, weight_sum = route(own, index, slot_weight)
    part = blur(image, psf_kernel[0])
    return reduce(part, weight_sum)


def solution(mesh):
    in_specs = (
        P("visit", "patch", None, None),
        P("visit", "patch", None, None),
        P("visit", "patch"),
        P("visit", "patch", None),
        P("visit", "patch", None),
        P("visit", "patch"),
        P("visit", None, None),
    )
    out_specs = P("patch", "visit")
    return jax.shard_map(
        on_device, mesh=mesh, in_specs=in_specs, out_specs=out_specs, check_vma=False
    )
```

```python
import math

import jax
import jax.numpy as jnp
from jax import lax
from jax.experimental import pallas as pl
from jax.experimental.pallas import tpu as pltpu
from jax.sharding import PartitionSpec as P

EDGE = 128
BLOCKS = 64
CAP = 16
KSIZE = 25
REACH = 12
GROUP = 8
CHUNK = 4
SLOT_COLS = 8
SLOT_ROWS = 8
ROWS = SLOT_ROWS * EDGE
COLS = SLOT_COLS * EDGE
HALO = 16
EXT_ROWS = ROWS + 2 * HALO
SEGS = 16
SEG_ROWS = ROWS // SEGS
PAIRS = SEG_ROWS // 2
STEPS = KSIZE // 2 + 1
EXT_PAIRS = PAIRS + STEPS - 1
SIDE = 2 * REACH
PACK = EDGE // SIDE
HALVES = -(-2 * STEPS // PACK)
DEPTH = STEPS * 2 * EDGE + HALVES * EDGE
TILE_ROWS = PAIRS * SEGS
F32 = jnp.float32
BF16 = jnp.bfloat16


def lanczos_weight(tap_offset):
    inside = jnp.abs(tap_offset) < 3.0
    safe_tap = jnp.where(inside, tap_offset, 1.5)
    value = (
        3.0
        * jnp.sin(math.pi * safe_tap)
        * jnp.sin(math.pi * safe_tap / 3.0)
        / (math.pi * math.pi * safe_tap * safe_tap)
    )
    return jnp.where(inside, value, 0.0)


def column_of(row):
    count = row.shape[1]
    down = lax.broadcasted_iota(jnp.int32, (count, count), 0)
    across = lax.broadcasted_iota(jnp.int32, (count, count), 1)
    spread = jnp.where(down == across, jnp.broadcast_to(row, (count, count)), 0.0)
    return jnp.sum(spread, axis=1, keepdims=True)


def toeplitz(row, rows):
    return pltpu.roll(jnp.broadcast_to(row, (rows, EDGE)), 0, 1, stride=1, stride_axis=0)


def build_taps(psf_ref, psf_rows, taps):
    for a in range(KSIZE):
        psf_rows[a : a + 1, :] = psf_ref[a]
    source = lax.broadcasted_iota(jnp.int32, (KSIZE, EDGE), 0)
    target = lax.broadcasted_iota(jnp.int32, (KSIZE, EDGE), 1)
    flip = jnp.where((target + source) % EDGE == 0, 1.0, 0.0).astype(BF16)
    flipped = jnp.dot(psf_rows[...].astype(BF16), flip, preferred_element_type=F32)
    centred = pltpu.roll(flipped, REACH, 1)
    down = lax.broadcasted_iota(jnp.int32, (EDGE, EDGE), 0)
    across = lax.broadcasted_iota(jnp.int32, (EDGE, EDGE), 1)
    near = jnp.abs(across - down) <= REACH
    beside = (down[:SIDE] < REACH) == (across[:SIDE] < EDGE // 2)

    def lanes(row_out):
        return slice(row_out * EDGE, (row_out + 1) * EDGE)

    for a in range(-1, KSIZE + 1):
        if 0 <= a < KSIZE:
            block = jnp.where(near, toeplitz(centred[a : a + 1], EDGE), 0.0).astype(BF16)
        else:
            block = jnp.zeros((EDGE, EDGE), BF16)
        for row_out in range(2):
            row_in = a + row_out
            if 0 <= row_in < 2 * STEPS:
                taps[row_in * EDGE : (row_in + 1) * EDGE, lanes(row_out)] = block
    for half in range(HALVES):
        for row_out in range(2):
            parts = []
            for i in range(PACK):
                a = PACK * half + i - row_out
                if 0 <= a < KSIZE:
                    parts.append(jnp.where(beside, toeplitz(flipped[a : a + 1], SIDE), 0.0))
                else:
                    parts.append(jnp.zeros((SIDE, EDGE), F32))
            parts.append(jnp.zeros((EDGE - PACK * SIDE, EDGE), F32))
            base = STEPS * 2 * EDGE + half * EDGE
            taps[base : base + EDGE, lanes(row_out)] = jnp.concatenate(parts, axis=0).astype(BF16)


def build_select(select):
    shape = (4 * EDGE, 2 * EDGE)
    source = lax.broadcasted_iota(jnp.int32, shape, 0)
    lane = lax.broadcasted_iota(jnp.int32, shape, 1)
    inner = lax.rem(lane, EDGE)
    q = lax.rem(inner, SIDE)
    wanted = jnp.where(q < REACH, EDGE - REACH + q, 2 * EDGE + q - REACH) + (lane - inner)
    hit = (source == wanted) & (inner < PACK * SIDE)
    select[...] = jnp.where(hit, 1.0, 0.0).astype(BF16)


def remote(src, dst, send_sem, recv_sem, **target):
    return pltpu.make_async_remote_copy(
        src_ref=src,
        dst_ref=dst,
        send_sem=send_sem,
        recv_sem=recv_sem,
        device_id=target,
        device_id_type=pl.DeviceIdType.MESH,
    )


def coadd_kernel(
    list_hbm,
    slot_hbm,
    offset_hbm,
    frac_hbm,
    inv_var_hbm,
    psf_hbm,
    blocks_hbm,
    out_ref,
    lists,
    slots,
    slot_vec,
    offset_vec,
    frac_vec,
    inv_var_vec,
    psf_vec,
    psf_rows,
    raw,
    row_taps,
    col_taps,
    weights,
    staying,
    staying_flat,
    index_mine,
    index_in,
    index_sum,
    index_flat,
    weight_mine,
    weight_in,
    weight_sum,
    weight_all,
    outgoing,
    held,
    wide,
    halo_out,
    halo_in,
    centre,
    edges,
    sides,
    select,
    taps,
    own_part,
    pair_out,
    pair_in,
    relay_out,
    relay_in,
    chip_out,
    chip_in,
    local_sem,
    block_send,
    block_recv,
    meta_send,
    meta_recv,
    halo_send,
    halo_recv,
    pair_send,
    pair_recv,
    relay_send,
    relay_recv,
    chip_send,
    chip_recv,
    weight_send,
    weight_recv,
):
    patch = lax.axis_index("patch")
    last = lax.axis_size("patch") - 1
    visit = lax.axis_index("visit")
    visits = lax.axis_size("visit")
    chips = visits // 2
    chip, core = visit // 2, lax.rem(visit, 2)
    partner = visit + 1 - 2 * core
    has_low, has_high = patch > 0, patch < last
    sides_of = (
        (has_low, jnp.maximum(patch - 1, 0)),
        (has_high, jnp.minimum(patch + 1, last)),
    )

    loads = [
        pltpu.make_async_copy(src, dst, local_sem.at[i])
        for i, (src, dst) in enumerate(
            (
                (offset_hbm, offset_vec),
                (frac_hbm, frac_vec),
                (inv_var_hbm, inv_var_vec),
                (list_hbm, lists),
                (slot_hbm, slots),
                (slot_hbm, slot_vec),
                (psf_hbm, psf_vec),
                (blocks_hbm, raw),
            )
        )
    ]
    for load in loads:
        load.start()

    barrier = pltpu.get_barrier_semaphore()
    for there, neighbour in sides_of:

        @pl.when(there)
        def greet():
            pl.semaphore_signal(
                barrier, inc=1, device_id={"patch": neighbour}, device_id_type=pl.DeviceIdType.MESH
            )

    for d in range(1, visits):
        pl.semaphore_signal(
            barrier,
            inc=1,
            device_id={"visit": lax.rem(visit + d, visits)},
            device_id_type=pl.DeviceIdType.MESH,
        )

    for load in loads[:3]:
        load.wait()
    shift_rows = column_of(offset_vec[0:1, :].astype(F32) + frac_vec[0:1, :].astype(F32))
    shift_cols = column_of(offset_vec[1:2, :].astype(F32) + frac_vec[1:2, :].astype(F32))
    lane_block = lax.broadcasted_iota(jnp.int32, (BLOCKS, EDGE), 1)
    signed = jnp.where(lane_block < EDGE // 2, lane_block, lane_block - EDGE).astype(F32)
    row_taps[...] = lanczos_weight(signed - shift_rows).astype(BF16).astype(F32)
    col_taps[...] = lanczos_weight(-signed - shift_cols).astype(BF16).astype(F32)
    weights[...] = jnp.broadcast_to(column_of(inv_var_vec[...].astype(F32)), (BLOCKS, EDGE))

    down = lax.broadcasted_iota(jnp.int32, (EDGE, EDGE), 0)
    across = lax.broadcasted_iota(jnp.int32, (EDGE, EDGE), 1)
    near = jnp.abs(down - across) < EDGE // 2

    def band(taps_ref, j):
        rolled = toeplitz(taps_ref[pl.ds(j, 1), :], EDGE)
        return jnp.where(near, rolled, 0.0).astype(BF16)

    def warped(j):
        first = jnp.dot(band(row_taps, j), raw[j], preferred_element_type=F32)
        second = jnp.dot(first.astype(BF16), band(col_taps, j), preferred_element_type=F32)
        return (second.astype(BF16).astype(F32) * weights[pl.ds(j, 1), :]).astype(BF16)

    def block_copy(side, chunk, neighbour):
        lands = 1 - side
        return remote(
            outgoing.at[side, pl.ds(chunk * CHUNK, CHUNK)],
            held.at[pl.ds(BLOCKS + lands * CAP + chunk * CHUNK, CHUNK)],
            block_send.at[side, chunk],
            block_recv.at[lands, chunk],
            patch=neighbour,
        )

    def meta_copy(side, kind, neighbour):
        lands = 1 - side
        src, dst = ((index_mine, index_in), (weight_mine, weight_in))[kind]
        return remote(
            src, dst.at[lands], meta_send.at[side, kind], meta_recv.at[lands, kind], patch=neighbour
        )

    def halo_copy(side, neighbour):
        lands = 1 - side
        return remote(
            halo_out.at[side], halo_in.at[lands], halo_send.at[side], halo_recv.at[lands], patch=neighbour
        )

    for load in loads[3:]:
        load.wait()
    pl.semaphore_wait(barrier, visits - 1 + has_low.astype(jnp.int32) + has_high.astype(jnp.int32))

    def leave(chunk, carry):
        for side in range(2):
            for i in range(CHUNK):
                t = chunk * CHUNK + i
                outgoing[side, t] = warped(jnp.maximum(lists[side, t], 0))
        for side, (there, neighbour) in enumerate(sides_of):

            @pl.when(there)
            def send():
                block_copy(side, chunk, neighbour).start()

        return carry

    lax.fori_loop(0, CAP // CHUNK, leave, 0)

    lane = lax.broadcasted_iota(jnp.int32, (1, EDGE), 1)

    def list_leaving(t, carry):
        leaving, index_low, index_high, weight_low, weight_high = carry
        found = []
        for side in range(2):
            j = lists[side, t]
            inside = jnp.maximum(j, 0)
            leaving = jnp.where(lane == j, 1, leaving)
            here = (lane == slots[0, inside]) & (jnp.broadcast_to(j, (1, EDGE)) >= 0)
            code = BLOCKS + (1 - side) * CAP + t + 1
            found.append((jnp.where(here, code, 0), jnp.where(here, weights[pl.ds(inside, 1), :], 0.0)))
        return (
            leaving,
            index_low + found[0][0],
            index_high + found[1][0],
            weight_low + found[0][1],
            weight_high + found[1][1],
        )

    zeros_i = jnp.zeros((1, EDGE), jnp.int32)
    zeros_f = jnp.zeros((1, EDGE), F32)
    leaving, index_low, index_high, weight_low, weight_high = lax.fori_loop(
        0, CAP, list_leaving, (zeros_i, zeros_i, zeros_i, zeros_f, zeros_f)
    )
    staying[...] = jnp.full((8, EDGE), EDGE, jnp.int32)
    staying[0:1, 0:BLOCKS] = jnp.where(leaving[:, 0:BLOCKS] > 0, EDGE, slot_vec[...])
    flat = pltpu.make_async_copy(staying, staying_flat, local_sem.at[8])
    flat.start()
    flat.wait()

    def list_staying(j, carry):
        index_own, weight_own = carry
        here = lane == staying_flat[0, j]
        return (
            index_own + jnp.where(here, j + 1, 0),
            weight_own + jnp.where(here, weights[pl.ds(j, 1), :], 0.0),
        )

    index_own, weight_own = lax.fori_loop(0, BLOCKS, list_staying, (zeros_i, zeros_f))
    index_mine[...] = jnp.zeros((8, EDGE), jnp.int32)
    weight_mine[...] = jnp.zeros((8, EDGE), F32)
    for k, (index, weight) in enumerate(
        ((index_own, weight_own), (index_low, weight_low), (index_high, weight_high))
    ):
        index_mine[k : k + 1, :] = index
        weight_mine[k : k + 1, :] = weight
    for side, (there, neighbour) in enumerate(sides_of):

        @pl.when(there)
        def send_meta():
            for kind in range(2):
                meta_copy(side, kind, neighbour).start()

        @pl.when(jnp.logical_not(there))
        def nothing_comes():
            index_in[side] = jnp.zeros((8, EDGE), jnp.int32)
            weight_in[side] = jnp.zeros((8, EDGE), F32)
            halo_in[side] = jnp.zeros((SLOT_COLS, HALO, EDGE), BF16)

    def warp_group(group, carry):
        for i in range(GROUP):
            j = group * GROUP + i
            held[j] = warped(j)
        return carry

    lax.fori_loop(0, BLOCKS // GROUP, warp_group, 0)

    build_taps(psf_vec, psf_rows, taps)
    build_select(select)
    blank = jnp.zeros((EXT_PAIRS, SEGS, 2 * EDGE), BF16)
    centre[0] = blank
    centre[SLOT_COLS + 1] = blank
    edges[EXT_PAIRS : EXT_PAIRS + 2] = jnp.zeros((2, SEGS, 2 * EDGE), F32)

    for side, (there, neighbour) in enumerate(sides_of):

        @pl.when(there)
        def meta_arrives():
            for kind in range(2):
                meta_copy(1 - side, kind, neighbour).wait_recv()

    index_sum[...] = jnp.zeros((8, EDGE), jnp.int32)
    found = index_mine[0:1, :] + index_in[0, 2:3, :] + index_in[1, 1:2, :]
    index_sum[0:1, :] = jnp.clip(found, 1, BLOCKS + 2 * CAP) - 1
    weight_sum[...] = jnp.zeros((8, EDGE), F32)
    weight_sum[0:1, :] = weight_mine[0:1, :] + weight_in[0, 2:3, :] + weight_in[1, 1:2, :]

    def weight_copy(d):
        return remote(
            weight_sum,
            weight_all.at[d - 1],
            weight_send.at[d - 1],
            weight_recv.at[d - 1],
            visit=lax.rem(visit + d, visits),
        )

    for d in range(1, visits):
        weight_copy(d).start()
    flat = pltpu.make_async_copy(index_sum, index_flat, local_sem.at[9])
    flat.start()
    flat.wait()
    for side, (there, neighbour) in enumerate(sides_of):

        @pl.when(there)
        def blocks_arrive():
            for chunk in range(CAP // CHUNK):
                block_copy(1 - side, chunk, neighbour).wait_recv()

    def put(slot_row, carry):
        for slot_col in range(SLOT_COLS):
            source = index_flat[0, slot_row * SLOT_COLS + slot_col]
            top = pl.multiple_of(HALO + slot_row * EDGE, HALO)
            wide[slot_col, pl.ds(top, EDGE), :] = held[source].astype(F32)
        return carry

    lax.fori_loop(0, 2, lambda i, carry: put(i * (SLOT_ROWS - 1), carry), 0)
    halo_out[0] = wide[:, HALO : 2 * HALO, :].astype(BF16)
    halo_out[1] = wide[:, ROWS : ROWS + HALO, :].astype(BF16)
    for side, (there, neighbour) in enumerate(sides_of):

        @pl.when(there)
        def send_halo():
            halo_copy(side, neighbour).start()

    lax.fori_loop(1, SLOT_ROWS - 1, put, 0)

    def to_pairs(g, carry):
        for row_in in range(2):
            start = 2 * g + (HALO - REACH) + row_in
            for w in range(SLOT_COLS):
                rows = wide[w, pl.ds(start, SEGS, stride=SEG_ROWS), :]
                centre[w + 1, g, :, row_in * EDGE : (row_in + 1) * EDGE] = rows.astype(BF16)
        return carry

    lax.fori_loop(REACH // 2, REACH // 2 + PAIRS, to_pairs, 0)
    for side, (there, neighbour) in enumerate(sides_of):

        @pl.when(there)
        def halo_arrives():
            halo_copy(1 - side, neighbour).wait_recv()

    wide[:, 0:HALO, :] = halo_in[0].astype(F32)
    wide[:, HALO + ROWS : EXT_ROWS, :] = halo_in[1].astype(F32)
    lax.fori_loop(0, REACH // 2, to_pairs, 0)
    lax.fori_loop(REACH // 2 + PAIRS, EXT_PAIRS, to_pairs, 0)

    lane_seg = lax.broadcasted_iota(jnp.int32, (SEGS, EDGE), 1)

    def side_columns(w, carry):
        both = jnp.concatenate(
            [centre[w + k].reshape(EXT_PAIRS * SEGS, 2 * EDGE) for k in (0, 2)], axis=1
        )
        placed = jnp.dot(both, select[...], preferred_element_type=F32)
        edges[0:EXT_PAIRS] = placed.reshape(EXT_PAIRS, SEGS, 2 * EDGE)

        def pack(i, inner):
            for k in range(4):
                g = i * 4 + k
                rows = [edges[g + n // 2, :, (n % 2) * EDGE : (n % 2 + 1) * EDGE] for n in range(PACK + 1)]
                for odd in range(2):
                    packed = rows[odd + PACK - 1]
                    for n in range(PACK - 2, -1, -1):
                        packed = jnp.where(lane_seg < (n + 1) * SIDE, rows[odd + n], packed)
                    sides[odd, w, g] = packed.astype(BF16)
            return inner

        lax.fori_loop(0, EXT_PAIRS // 4, pack, 0)
        return carry

    lax.fori_loop(0, SLOT_COLS, side_columns, 0)

    def pair_copy(k):
        return remote(pair_out.at[k], pair_in.at[k], pair_send.at[k], pair_recv.at[k], visit=partner)

    ahead = 2 * lax.rem(chip + 1, chips) + core
    behind = 2 * lax.rem(chip + chips - 1, chips) + core
    ways = (ahead, behind)

    def relay_copy(way):
        return remote(
            relay_out.at[way], relay_in.at[way], relay_send.at[way], relay_recv.at[way], visit=ways[way]
        )

    def chip_copy(way):
        return remote(
            chip_out.at[way], chip_in.at[way], chip_send.at[way], chip_recv.at[way], visit=ways[way]
        )

    def total(k, half, r):
        rows = pl.ds(pl.multiple_of(half * TILE_ROWS + r * EDGE, EDGE), EDGE)
        return rows, own_part[rows, :] + pair_in[k, rows, :].astype(F32)

    strips = TILE_ROWS // EDGE

    def tile_step(i, carry):
        k = i // 2
        mine = lax.rem(i, 2)
        distance = jnp.where(k == 0, 2, jnp.where(k == 1, 1, jnp.where(k == 2, chips - 1, 0)))
        to_core = jnp.where(mine == 1, core, 1 - core)
        w = 2 * lax.rem(chip + distance, chips) + to_core
        columns = [
            centre[w + 1, t : t + PAIRS].reshape(TILE_ROWS, 2 * EDGE) for t in range(STEPS)
        ]
        for half in range(HALVES):
            row = PACK * half
            columns.append(sides[row % 2, w, row // 2 : row // 2 + PAIRS].reshape(TILE_ROWS, EDGE))
        acc = jnp.dot(jnp.concatenate(columns, axis=1), taps[...], preferred_element_type=F32)

        @pl.when(mine == 0)
        def for_partner():
            for row_out in range(2):
                pair_out[k, row_out * TILE_ROWS : (row_out + 1) * TILE_ROWS, :] = acc[
                    :, row_out * EDGE : (row_out + 1) * EDGE
                ].astype(BF16)
            pair_copy(k).start()

        @pl.when(mine == 1)
        def for_this_core():
            for row_out in range(2):
                own_part[row_out * TILE_ROWS : (row_out + 1) * TILE_ROWS, :] = acc[
                    :, row_out * EDGE : (row_out + 1) * EDGE
                ]
            pair_copy(k).wait_recv()

            @pl.when(k == 0)
            def opposite():
                for way in range(2):

                    def add(r, inner):
                        _, value = total(k, way, r)
                        relay_out[way, pl.ds(pl.multiple_of(r * EDGE, EDGE), EDGE), :] = value.astype(BF16)
                        return inner

                    lax.fori_loop(0, strips, add, 0)
                    relay_copy(way).start()

            for way in range(2):

                @pl.when(k == 1 + way)
                def beside():
                    relay_copy(way).wait_recv()
                    for half in range(2):

                        def add(r, inner):
                            rows, value = total(k, half, r)
                            if half == way:
                                value = value + relay_in[way, pl.ds(pl.multiple_of(r * EDGE, EDGE), EDGE), :].astype(F32)
                            chip_out[way, rows, :] = value.astype(BF16)
                            return inner

                        lax.fori_loop(0, strips, add, 0)
                    chip_copy(way).start()

        return carry

    lax.fori_loop(0, SLOT_COLS, tile_step, 0)

    for d in range(1, visits):
        weight_copy(d).wait_recv()
    denom = weight_sum[0:1, :]
    for d in range(1, visits):
        denom = denom + weight_all[d - 1, 0:1, :]
    row_seg = lax.broadcasted_iota(jnp.int32, (SEGS, EDGE), 0)
    wanted = (row_seg // 2) * SLOT_COLS + visit
    denom = jnp.sum(
        jnp.where(lane_seg == wanted, jnp.broadcast_to(denom, (SEGS, EDGE)), 0.0), axis=1, keepdims=True
    )
    denom = jnp.broadcast_to(denom, (SEGS, EDGE))
    for way in range(2):
        chip_copy(way).wait_recv()

    def finish(g, carry):
        for row_out in range(2):
            rows = pl.ds(pl.multiple_of(row_out * TILE_ROWS + g * SEGS, SEGS), SEGS)
            value = own_part[rows, :] + pair_in[chips - 1, rows, :].astype(F32)
            for way in range(2):
                value = value + chip_in[way, rows, :].astype(F32)
            out_ref[pl.ds(2 * g + row_out, SEGS, stride=SEG_ROWS), :] = value / denom
        return carry

    lax.fori_loop(0, PAIRS, finish, 0)

    for side, (there, neighbour) in enumerate(sides_of):

        @pl.when(there)
        def sent():
            for chunk in range(CAP // CHUNK):
                block_copy(side, chunk, neighbour).wait_send()
            for kind in range(2):
                meta_copy(side, kind, neighbour).wait_send()
            halo_copy(side, neighbour).wait_send()

    for k in range(chips):
        pair_copy(k).wait_send()
    for way in range(2):
        relay_copy(way).wait_send()
        chip_copy(way).wait_send()
    for d in range(1, visits):
        weight_copy(d).wait_send()


def coadd(send_list, block_slot, block_offset, block_frac, inv_var, psf, blocks):
    visits = lax.axis_size("visit")
    chips = visits // 2
    hbm = pl.BlockSpec(memory_space=pl.ANY)
    dma = pltpu.SemaphoreType.DMA
    return pl.pallas_call(
        coadd_kernel,
        out_shape=jax.ShapeDtypeStruct((ROWS, EDGE), F32),
        in_specs=[hbm] * 7,
        out_specs=pl.BlockSpec(memory_space=pltpu.VMEM),
        scratch_shapes=[
            pltpu.SMEM((2, CAP), jnp.int32),
            pltpu.SMEM((1, BLOCKS), jnp.int32),
            pltpu.VMEM((1, BLOCKS), jnp.int32),
            pltpu.VMEM((2, BLOCKS), jnp.int32),
            pltpu.VMEM((2, BLOCKS), BF16),
            pltpu.VMEM((1, BLOCKS), BF16),
            pltpu.VMEM((KSIZE, 1, KSIZE), F32),
            pltpu.VMEM((KSIZE, KSIZE), F32),
            pltpu.VMEM((BLOCKS, EDGE, EDGE), BF16),
            pltpu.VMEM((BLOCKS, EDGE), F32),
            pltpu.VMEM((BLOCKS, EDGE), F32),
            pltpu.VMEM((BLOCKS, EDGE), F32),
            pltpu.VMEM((8, EDGE), jnp.int32),
            pltpu.SMEM((8, EDGE), jnp.int32),
            pltpu.VMEM((8, EDGE), jnp.int32),
            pltpu.VMEM((2, 8, EDGE), jnp.int32),
            pltpu.VMEM((8, EDGE), jnp.int32),
            pltpu.SMEM((8, EDGE), jnp.int32),
            pltpu.VMEM((8, EDGE), F32),
            pltpu.VMEM((2, 8, EDGE), F32),
            pltpu.VMEM((8, EDGE), F32),
            pltpu.VMEM((visits - 1, 8, EDGE), F32),
            pltpu.VMEM((2, CAP, EDGE, EDGE), BF16),
            pltpu.VMEM((BLOCKS + 2 * CAP, EDGE, EDGE), BF16),
            pltpu.VMEM((SLOT_COLS, EXT_ROWS, EDGE), F32),
            pltpu.VMEM((2, SLOT_COLS, HALO, EDGE), BF16),
            pltpu.VMEM((2, SLOT_COLS, HALO, EDGE), BF16),
            pltpu.VMEM((SLOT_COLS + 2, EXT_PAIRS, SEGS, 2 * EDGE), BF16),
            pltpu.VMEM((EXT_PAIRS + 2, SEGS, 2 * EDGE), F32),
            pltpu.VMEM((2, SLOT_COLS, EXT_PAIRS, SEGS, EDGE), BF16),
            pltpu.VMEM((4 * EDGE, 2 * EDGE), BF16),
            pltpu.VMEM((DEPTH, 2 * EDGE), BF16),
            pltpu.VMEM((ROWS, EDGE), F32),
            pltpu.VMEM((chips, ROWS, EDGE), BF16),
            pltpu.VMEM((chips, ROWS, EDGE), BF16),
            pltpu.VMEM((2, TILE_ROWS, EDGE), BF16),
            pltpu.VMEM((2, TILE_ROWS, EDGE), BF16),
            pltpu.VMEM((2, ROWS, EDGE), BF16),
            pltpu.VMEM((2, ROWS, EDGE), BF16),
            dma((10,)),
            dma((2, CAP // CHUNK)),
            dma((2, CAP // CHUNK)),
            dma((2, 2)),
            dma((2, 2)),
            dma((2,)),
            dma((2,)),
            dma((chips,)),
            dma((chips,)),
            dma((2,)),
            dma((2,)),
            dma((2,)),
            dma((2,)),
            dma((visits - 1,)),
            dma((visits - 1,)),
        ],
        compiler_params=pltpu.CompilerParams(
            collective_id=0, has_side_effects=True, vmem_limit_bytes=56 << 20
        ),
        name="coadd",
    )(send_list, block_slot, block_offset, block_frac, inv_var, psf, blocks)


def on_device(blocks, send_list, block_slot, block_offset, block_frac, inv_var, psf_kernel):
    return coadd(
        send_list[0, 0],
        block_slot,
        block_offset[0].T,
        block_frac[0].T,
        inv_var,
        jnp.transpose(psf_kernel, (1, 0, 2)),
        blocks[0],
    )


def solution(mesh):
    in_specs = (
        P("visit", "patch", None, None),
        P("visit", "patch", None, None),
        P("visit", "patch"),
        P("visit", "patch", None),
        P("visit", "patch", None),
        P("visit", "patch"),
        P("visit", None, None),
    )
    out_specs = P("patch", "visit")
    return jax.shard_map(
        on_device, mesh=mesh, in_specs=in_specs, out_specs=out_specs, check_vma=False
    )
```

```python
import math

import jax
import jax.numpy as jnp
from jax import lax
from jax.experimental import pallas as pl
from jax.experimental.pallas import tpu as pltpu
from jax.sharding import PartitionSpec as P

EDGE = 128
BLOCKS = 64
CAP = 16
KSIZE = 25
REACH = 12
GROUP = 8
CHUNK = 4
SLOT_COLS = 8
SLOT_ROWS = 8
ROWS = SLOT_ROWS * EDGE
COLS = SLOT_COLS * EDGE
HALO = 16
EXT_ROWS = ROWS + 2 * HALO
SEGS = 16
SEG_ROWS = ROWS // SEGS
PAIRS = SEG_ROWS // 2
STEPS = KSIZE // 2 + 1
EXT_PAIRS = PAIRS + STEPS - 1
SIDE = 2 * REACH
PACK = EDGE // SIDE
HALVES = -(-2 * STEPS // PACK)
DEPTH = STEPS * 2 * EDGE + HALVES * EDGE
HALF_PAIRS = PAIRS // 2
HALF_ROWS = ROWS // 2
F32 = jnp.float32
BF16 = jnp.bfloat16


def lanczos_weight(tap_offset):
    inside = jnp.abs(tap_offset) < 3.0
    safe_tap = jnp.where(inside, tap_offset, 1.5)
    value = (
        3.0
        * jnp.sin(math.pi * safe_tap)
        * jnp.sin(math.pi * safe_tap / 3.0)
        / (math.pi * math.pi * safe_tap * safe_tap)
    )
    return jnp.where(inside, value, 0.0)


def column_of(row):
    count = row.shape[1]
    down = lax.broadcasted_iota(jnp.int32, (count, count), 0)
    across = lax.broadcasted_iota(jnp.int32, (count, count), 1)
    spread = jnp.where(down == across, jnp.broadcast_to(row, (count, count)), 0.0)
    return jnp.sum(spread, axis=1, keepdims=True)


def toeplitz(row, rows):
    return pltpu.roll(jnp.broadcast_to(row, (rows, EDGE)), 0, 1, stride=1, stride_axis=0)


def build_taps(psf_ref, psf_rows, taps):
    for a in range(KSIZE):
        psf_rows[a : a + 1, :] = psf_ref[a]
    source = lax.broadcasted_iota(jnp.int32, (KSIZE, EDGE), 0)
    target = lax.broadcasted_iota(jnp.int32, (KSIZE, EDGE), 1)
    flip = jnp.where((target + source) % EDGE == 0, 1.0, 0.0).astype(BF16)
    flipped = jnp.dot(psf_rows[...].astype(BF16), flip, preferred_element_type=F32)
    centred = pltpu.roll(flipped, REACH, 1)
    down = lax.broadcasted_iota(jnp.int32, (EDGE, EDGE), 0)
    across = lax.broadcasted_iota(jnp.int32, (EDGE, EDGE), 1)
    near = jnp.abs(across - down) <= REACH
    beside = (down[:SIDE] < REACH) == (across[:SIDE] < EDGE // 2)

    def lanes(row_out):
        return slice(row_out * EDGE, (row_out + 1) * EDGE)

    for a in range(-1, KSIZE + 1):
        if 0 <= a < KSIZE:
            block = jnp.where(near, toeplitz(centred[a : a + 1], EDGE), 0.0).astype(BF16)
        else:
            block = jnp.zeros((EDGE, EDGE), BF16)
        for row_out in range(2):
            row_in = a + row_out
            if 0 <= row_in < 2 * STEPS:
                taps[row_in * EDGE : (row_in + 1) * EDGE, lanes(row_out)] = block
    for half in range(HALVES):
        for row_out in range(2):
            parts = []
            for i in range(PACK):
                a = PACK * half + i - row_out
                if 0 <= a < KSIZE:
                    parts.append(jnp.where(beside, toeplitz(flipped[a : a + 1], SIDE), 0.0))
                else:
                    parts.append(jnp.zeros((SIDE, EDGE), F32))
            parts.append(jnp.zeros((EDGE - PACK * SIDE, EDGE), F32))
            base = STEPS * 2 * EDGE + half * EDGE
            taps[base : base + EDGE, lanes(row_out)] = jnp.concatenate(parts, axis=0).astype(BF16)


def build_select(select):
    shape = (4 * EDGE, 2 * EDGE)
    source = lax.broadcasted_iota(jnp.int32, shape, 0)
    lane = lax.broadcasted_iota(jnp.int32, shape, 1)
    inner = lax.rem(lane, EDGE)
    q = lax.rem(inner, SIDE)
    wanted = jnp.where(q < REACH, EDGE - REACH + q, 2 * EDGE + q - REACH) + (lane - inner)
    hit = (source == wanted) & (inner < PACK * SIDE)
    select[...] = jnp.where(hit, 1.0, 0.0).astype(BF16)


def remote(src, dst, send_sem, recv_sem, **target):
    return pltpu.make_async_remote_copy(
        src_ref=src,
        dst_ref=dst,
        send_sem=send_sem,
        recv_sem=recv_sem,
        device_id=target,
        device_id_type=pl.DeviceIdType.MESH,
    )


def coadd_kernel(
    list_hbm,
    slot_hbm,
    offset_hbm,
    frac_hbm,
    inv_var_hbm,
    psf_hbm,
    blocks_hbm,
    out_ref,
    lists,
    slots,
    slot_vec,
    offset_vec,
    frac_vec,
    inv_var_vec,
    psf_vec,
    psf_rows,
    raw,
    row_taps,
    col_taps,
    weights,
    staying,
    staying_flat,
    index_mine,
    index_in,
    index_sum,
    index_flat,
    weight_mine,
    weight_in,
    weight_sum,
    weight_all,
    outgoing,
    held,
    wide,
    halo_out,
    halo_in,
    centre,
    edges,
    sides,
    select,
    taps,
    own_part,
    pair_out,
    pair_in,
    chip_out,
    chip_in,
    local_sem,
    block_send,
    block_recv,
    meta_send,
    meta_recv,
    halo_send,
    halo_recv,
    pair_send,
    pair_recv,
    chip_send,
    chip_recv,
    weight_send,
    weight_recv,
):
    patch = lax.axis_index("patch")
    last = lax.axis_size("patch") - 1
    visit = lax.axis_index("visit")
    visits = lax.axis_size("visit")
    chips = visits // 2
    chip, core = visit // 2, lax.rem(visit, 2)
    partner = visit + 1 - 2 * core
    has_low, has_high = patch > 0, patch < last
    sides_of = (
        (has_low, jnp.maximum(patch - 1, 0)),
        (has_high, jnp.minimum(patch + 1, last)),
    )

    loads = [
        pltpu.make_async_copy(src, dst, local_sem.at[i])
        for i, (src, dst) in enumerate(
            (
                (offset_hbm, offset_vec),
                (frac_hbm, frac_vec),
                (inv_var_hbm, inv_var_vec),
                (list_hbm, lists),
                (slot_hbm, slots),
                (slot_hbm, slot_vec),
                (psf_hbm, psf_vec),
                (blocks_hbm, raw),
            )
        )
    ]
    for load in loads:
        load.start()

    barrier = pltpu.get_barrier_semaphore()
    for there, neighbour in sides_of:

        @pl.when(there)
        def greet():
            pl.semaphore_signal(
                barrier, inc=1, device_id={"patch": neighbour}, device_id_type=pl.DeviceIdType.MESH
            )

    for d in range(1, visits):
        pl.semaphore_signal(
            barrier,
            inc=1,
            device_id={"visit": lax.rem(visit + d, visits)},
            device_id_type=pl.DeviceIdType.MESH,
        )

    for load in loads[:3]:
        load.wait()
    shift_rows = column_of(offset_vec[0:1, :].astype(F32) + frac_vec[0:1, :].astype(F32))
    shift_cols = column_of(offset_vec[1:2, :].astype(F32) + frac_vec[1:2, :].astype(F32))
    lane_block = lax.broadcasted_iota(jnp.int32, (BLOCKS, EDGE), 1)
    signed = jnp.where(lane_block < EDGE // 2, lane_block, lane_block - EDGE).astype(F32)
    row_taps[...] = lanczos_weight(signed - shift_rows).astype(BF16).astype(F32)
    col_taps[...] = lanczos_weight(-signed - shift_cols).astype(BF16).astype(F32)
    weights[...] = jnp.broadcast_to(column_of(inv_var_vec[...].astype(F32)), (BLOCKS, EDGE))

    down = lax.broadcasted_iota(jnp.int32, (EDGE, EDGE), 0)
    across = lax.broadcasted_iota(jnp.int32, (EDGE, EDGE), 1)
    near = jnp.abs(down - across) < EDGE // 2

    def band(taps_ref, j):
        rolled = toeplitz(taps_ref[pl.ds(j, 1), :], EDGE)
        return jnp.where(near, rolled, 0.0).astype(BF16)

    def warped(j):
        first = jnp.dot(band(row_taps, j), raw[j], preferred_element_type=F32)
        second = jnp.dot(first.astype(BF16), band(col_taps, j), preferred_element_type=F32)
        return (second.astype(BF16).astype(F32) * weights[pl.ds(j, 1), :]).astype(BF16)

    def block_copy(side, chunk, neighbour):
        lands = 1 - side
        return remote(
            outgoing.at[side, pl.ds(chunk * CHUNK, CHUNK)],
            held.at[pl.ds(BLOCKS + lands * CAP + chunk * CHUNK, CHUNK)],
            block_send.at[side, chunk],
            block_recv.at[lands, chunk],
            patch=neighbour,
        )

    def meta_copy(side, kind, neighbour):
        lands = 1 - side
        src, dst = ((index_mine, index_in), (weight_mine, weight_in))[kind]
        return remote(
            src, dst.at[lands], meta_send.at[side, kind], meta_recv.at[lands, kind], patch=neighbour
        )

    def halo_copy(side, neighbour):
        lands = 1 - side
        return remote(
            halo_out.at[side], halo_in.at[lands], halo_send.at[side], halo_recv.at[lands], patch=neighbour
        )

    for load in loads[3:]:
        load.wait()
    pl.semaphore_wait(barrier, visits - 1 + has_low.astype(jnp.int32) + has_high.astype(jnp.int32))

    def leave(chunk, carry):
        for side in range(2):
            for i in range(CHUNK):
                t = chunk * CHUNK + i
                outgoing[side, t] = warped(jnp.maximum(lists[side, t], 0))
        for side, (there, neighbour) in enumerate(sides_of):

            @pl.when(there)
            def send():
                block_copy(side, chunk, neighbour).start()

        return carry

    lax.fori_loop(0, CAP // CHUNK, leave, 0)

    lane = lax.broadcasted_iota(jnp.int32, (1, EDGE), 1)

    def list_leaving(t, carry):
        leaving, index_low, index_high, weight_low, weight_high = carry
        found = []
        for side in range(2):
            j = lists[side, t]
            inside = jnp.maximum(j, 0)
            leaving = jnp.where(lane == j, 1, leaving)
            here = (lane == slots[0, inside]) & (jnp.broadcast_to(j, (1, EDGE)) >= 0)
            code = BLOCKS + (1 - side) * CAP + t + 1
            found.append((jnp.where(here, code, 0), jnp.where(here, weights[pl.ds(inside, 1), :], 0.0)))
        return (
            leaving,
            index_low + found[0][0],
            index_high + found[1][0],
            weight_low + found[0][1],
            weight_high + found[1][1],
        )

    zeros_i = jnp.zeros((1, EDGE), jnp.int32)
    zeros_f = jnp.zeros((1, EDGE), F32)
    leaving, index_low, index_high, weight_low, weight_high = lax.fori_loop(
        0, CAP, list_leaving, (zeros_i, zeros_i, zeros_i, zeros_f, zeros_f)
    )
    staying[...] = jnp.full((8, EDGE), EDGE, jnp.int32)
    staying[0:1, 0:BLOCKS] = jnp.where(leaving[:, 0:BLOCKS] > 0, EDGE, slot_vec[...])
    flat = pltpu.make_async_copy(staying, staying_flat, local_sem.at[8])
    flat.start()
    flat.wait()

    def list_staying(j, carry):
        index_own, weight_own = carry
        here = lane == staying_flat[0, j]
        return (
            index_own + jnp.where(here, j + 1, 0),
            weight_own + jnp.where(here, weights[pl.ds(j, 1), :], 0.0),
        )

    index_own, weight_own = lax.fori_loop(0, BLOCKS, list_staying, (zeros_i, zeros_f))
    index_mine[...] = jnp.zeros((8, EDGE), jnp.int32)
    weight_mine[...] = jnp.zeros((8, EDGE), F32)
    for k, (index, weight) in enumerate(
        ((index_own, weight_own), (index_low, weight_low), (index_high, weight_high))
    ):
        index_mine[k : k + 1, :] = index
        weight_mine[k : k + 1, :] = weight
    for side, (there, neighbour) in enumerate(sides_of):

        @pl.when(there)
        def send_meta():
            for kind in range(2):
                meta_copy(side, kind, neighbour).start()

        @pl.when(jnp.logical_not(there))
        def nothing_comes():
            index_in[side] = jnp.zeros((8, EDGE), jnp.int32)
            weight_in[side] = jnp.zeros((8, EDGE), F32)
            halo_in[side] = jnp.zeros((SLOT_COLS, HALO, EDGE), BF16)

    def warp_group(group, carry):
        for i in range(GROUP):
            j = group * GROUP + i
            held[j] = warped(j)
        return carry

    lax.fori_loop(0, BLOCKS // GROUP, warp_group, 0)

    build_taps(psf_vec, psf_rows, taps)
    build_select(select)
    blank = jnp.zeros((EXT_PAIRS, SEGS, 2 * EDGE), BF16)
    centre[0] = blank
    centre[SLOT_COLS + 1] = blank
    edges[EXT_PAIRS : EXT_PAIRS + 2] = jnp.zeros((2, SEGS, 2 * EDGE), BF16)

    for side, (there, neighbour) in enumerate(sides_of):

        @pl.when(there)
        def meta_arrives():
            for kind in range(2):
                meta_copy(1 - side, kind, neighbour).wait_recv()

    index_sum[...] = jnp.zeros((8, EDGE), jnp.int32)
    found = index_mine[0:1, :] + index_in[0, 2:3, :] + index_in[1, 1:2, :]
    index_sum[0:1, :] = jnp.clip(found, 1, BLOCKS + 2 * CAP) - 1
    weight_sum[...] = jnp.zeros((8, EDGE), F32)
    weight_sum[0:1, :] = weight_mine[0:1, :] + weight_in[0, 2:3, :] + weight_in[1, 1:2, :]

    def weight_copy(d):
        return remote(
            weight_sum,
            weight_all.at[d - 1],
            weight_send.at[d - 1],
            weight_recv.at[d - 1],
            visit=lax.rem(visit + d, visits),
        )

    for d in range(1, visits):
        weight_copy(d).start()
    flat = pltpu.make_async_copy(index_sum, index_flat, local_sem.at[9])
    flat.start()
    flat.wait()
    for side, (there, neighbour) in enumerate(sides_of):

        @pl.when(there)
        def blocks_arrive():
            for chunk in range(CAP // CHUNK):
                block_copy(1 - side, chunk, neighbour).wait_recv()

    def put(slot_row, carry):
        for slot_col in range(SLOT_COLS):
            source = index_flat[0, slot_row * SLOT_COLS + slot_col]
            top = pl.multiple_of(HALO + slot_row * EDGE, HALO)
            wide[slot_col, pl.ds(top, EDGE), :] = held[source].astype(F32)
        return carry

    lax.fori_loop(0, 2, lambda i, carry: put(i * (SLOT_ROWS - 1), carry), 0)
    halo_out[0] = wide[:, HALO : 2 * HALO, :].astype(BF16)
    halo_out[1] = wide[:, ROWS : ROWS + HALO, :].astype(BF16)
    for side, (there, neighbour) in enumerate(sides_of):

        @pl.when(there)
        def send_halo():
            halo_copy(side, neighbour).start()

    lax.fori_loop(1, SLOT_ROWS - 1, put, 0)

    def to_pairs(g, carry):
        for row_in in range(2):
            start = 2 * g + (HALO - REACH) + row_in
            for w in range(SLOT_COLS):
                rows = wide[w, pl.ds(start, SEGS, stride=SEG_ROWS), :]
                centre[w + 1, g, :, row_in * EDGE : (row_in + 1) * EDGE] = rows.astype(BF16)
        return carry

    lax.fori_loop(REACH // 2, REACH // 2 + PAIRS, to_pairs, 0)
    for side, (there, neighbour) in enumerate(sides_of):

        @pl.when(there)
        def halo_arrives():
            halo_copy(1 - side, neighbour).wait_recv()

    wide[:, 0:HALO, :] = halo_in[0].astype(F32)
    wide[:, HALO + ROWS : EXT_ROWS, :] = halo_in[1].astype(F32)
    lax.fori_loop(0, REACH // 2, to_pairs, 0)
    lax.fori_loop(REACH // 2 + PAIRS, EXT_PAIRS, to_pairs, 0)

    lane_seg = lax.broadcasted_iota(jnp.int32, (SEGS, EDGE), 1)

    lane_pack = lane_seg.astype(BF16)

    def side_columns(w, carry):
        both = jnp.concatenate(
            [centre[w + k].reshape(EXT_PAIRS * SEGS, 2 * EDGE) for k in (0, 2)], axis=1
        )
        placed = jnp.dot(both, select[...], preferred_element_type=F32)
        edges[0:EXT_PAIRS] = placed.astype(BF16).reshape(EXT_PAIRS, SEGS, 2 * EDGE)

        def pack(i, inner):
            for k in range(4):
                g = i * 4 + k
                rows = [edges[g + n // 2, :, (n % 2) * EDGE : (n % 2 + 1) * EDGE] for n in range(PACK + 1)]
                for odd in range(2):
                    packed = rows[odd + PACK - 1]
                    for n in range(PACK - 2, -1, -1):
                        packed = jnp.where(lane_pack < (n + 1) * SIDE, rows[odd + n], packed)
                    sides[odd, w, g] = packed
            return inner

        lax.fori_loop(0, EXT_PAIRS // 4, pack, 0)
        return carry

    lax.fori_loop(0, SLOT_COLS, side_columns, 0)

    def pair_copy(k):
        return remote(pair_out.at[k], pair_in.at[k], pair_send.at[k], pair_recv.at[k], visit=partner)

    ways = (
        2 * lax.rem(chip + 1, chips) + core,
        2 * lax.rem(chip + chips - 1, chips) + core,
    )

    def chip_copy(k, way):
        return remote(
            chip_out.at[k, way],
            chip_in.at[k, way],
            chip_send.at[k, way],
            chip_recv.at[k, way],
            visit=ways[way],
        )

    def half_tile(w, half):
        first = half * HALF_PAIRS
        columns = [
            centre[w + 1, pl.ds(first + t, HALF_PAIRS)].reshape(HALF_ROWS // 2, 2 * EDGE) for t in range(STEPS)
        ]
        for part in range(HALVES):
            row = PACK * part
            columns.append(
                sides[row % 2, w, pl.ds(first + row // 2, HALF_PAIRS)].reshape(HALF_ROWS // 2, EDGE)
            )
        return columns

    strip = 2 * EDGE

    def tile_step(i, carry):
        k = i // 2
        mine = lax.rem(i, 2)
        to_core = jnp.where(mine == 1, core, 1 - core)
        ahead = jnp.where(k == 0, 2, jnp.where(k == chips - 1, 0, 1))
        behind = jnp.where(k == 0, 2, jnp.where(k == chips - 1, 0, chips - 1))
        half = jnp.where(k == 1, 1, 0)
        upper = half_tile(2 * lax.rem(chip + ahead, chips) + to_core, half)
        lower = half_tile(2 * lax.rem(chip + behind, chips) + to_core, 1 - half)
        both = jnp.concatenate(
            [jnp.concatenate([a, b], axis=0) for a, b in zip(upper, lower)], axis=1
        )
        acc = jnp.dot(both, taps[...], preferred_element_type=F32)

        def pieces():
            for way in range(2):
                for row_out in range(2):
                    first = way * HALF_ROWS + row_out * (HALF_ROWS // 2)
                    yield slice(first, first + HALF_ROWS // 2), acc[
                        way * (HALF_ROWS // 2) : (way + 1) * (HALF_ROWS // 2),
                        row_out * EDGE : (row_out + 1) * EDGE,
                    ]

        @pl.when(mine == 0)
        def for_partner():
            for rows, value in pieces():
                pair_out[k, rows, :] = value.astype(BF16)
            pair_copy(k).start()

        @pl.when(mine == 1)
        def for_this_core():
            for rows, value in pieces():
                own_part[rows, :] = value
            pair_copy(k).wait_recv()

            def send(extra):
                for way in range(2):
                    if extra:
                        chip_copy(0, way).wait_recv()

                    def add(r, inner):
                        here = pl.ds(pl.multiple_of(r * strip, strip), strip)
                        rows = pl.ds(pl.multiple_of(way * HALF_ROWS + r * strip, strip), strip)
                        value = own_part[rows, :] + pair_in[k, rows, :].astype(F32)
                        if extra:
                            value = value + chip_in[0, way, here, :].astype(F32)
                        chip_out[k, way, here, :] = value.astype(BF16)
                        return inner

                    lax.fori_loop(0, HALF_ROWS // strip, add, 0)
                    chip_copy(k, way).start()

            @pl.when(k < 2)
            def plain():
                send(False)

            @pl.when(k == 2)
            def relayed():
                send(True)

        return carry

    lax.fori_loop(0, SLOT_COLS, tile_step, 0)

    for d in range(1, visits):
        weight_copy(d).wait_recv()
    denom = weight_sum[0:1, :]
    for d in range(1, visits):
        denom = denom + weight_all[d - 1, 0:1, :]
    row_seg = lax.broadcasted_iota(jnp.int32, (SEGS, EDGE), 0)
    wanted = (row_seg // 2) * SLOT_COLS + visit
    denom = jnp.sum(
        jnp.where(lane_seg == wanted, jnp.broadcast_to(denom, (SEGS, EDGE)), 0.0), axis=1, keepdims=True
    )
    denom = jnp.broadcast_to(denom, (SEGS, EDGE))
    for k in (1, 2):
        for way in range(2):
            chip_copy(k, way).wait_recv()

    def finish(g, carry):
        for half in range(2):
            for row_out in range(2):
                base = row_out * (HALF_ROWS // 2) + g * SEGS
                here = pl.ds(pl.multiple_of(base, SEGS), SEGS)
                rows = pl.ds(pl.multiple_of(half * HALF_ROWS + base, SEGS), SEGS)
                value = own_part[rows, :] + pair_in[chips - 1, rows, :].astype(F32)
                value = value + chip_in[1, 1 - half, here, :].astype(F32)
                value = value + chip_in[2, half, here, :].astype(F32)
                start = 2 * (half * HALF_PAIRS + g) + row_out
                out_ref[pl.ds(start, SEGS, stride=SEG_ROWS), :] = value / denom
        return carry

    lax.fori_loop(0, HALF_PAIRS, finish, 0)

    for side, (there, neighbour) in enumerate(sides_of):

        @pl.when(there)
        def sent():
            for chunk in range(CAP // CHUNK):
                block_copy(side, chunk, neighbour).wait_send()
            for kind in range(2):
                meta_copy(side, kind, neighbour).wait_send()
            halo_copy(side, neighbour).wait_send()

    for k in range(chips):
        pair_copy(k).wait_send()
    for k in range(chips - 1):
        for way in range(2):
            chip_copy(k, way).wait_send()
    for d in range(1, visits):
        weight_copy(d).wait_send()


def coadd(send_list, block_slot, block_offset, block_frac, inv_var, psf, blocks):
    visits = lax.axis_size("visit")
    chips = visits // 2
    hbm = pl.BlockSpec(memory_space=pl.ANY)
    dma = pltpu.SemaphoreType.DMA
    return pl.pallas_call(
        coadd_kernel,
        out_shape=jax.ShapeDtypeStruct((ROWS, EDGE), F32),
        in_specs=[hbm] * 7,
        out_specs=pl.BlockSpec(memory_space=pltpu.VMEM),
        scratch_shapes=[
            pltpu.SMEM((2, CAP), jnp.int32),
            pltpu.SMEM((1, BLOCKS), jnp.int32),
            pltpu.VMEM((1, BLOCKS), jnp.int32),
            pltpu.VMEM((2, BLOCKS), jnp.int32),
            pltpu.VMEM((2, BLOCKS), BF16),
            pltpu.VMEM((1, BLOCKS), BF16),
            pltpu.VMEM((KSIZE, 1, KSIZE), F32),
            pltpu.VMEM((KSIZE, KSIZE), F32),
            pltpu.VMEM((BLOCKS, EDGE, EDGE), BF16),
            pltpu.VMEM((BLOCKS, EDGE), F32),
            pltpu.VMEM((BLOCKS, EDGE), F32),
            pltpu.VMEM((BLOCKS, EDGE), F32),
            pltpu.VMEM((8, EDGE), jnp.int32),
            pltpu.SMEM((8, EDGE), jnp.int32),
            pltpu.VMEM((8, EDGE), jnp.int32),
            pltpu.VMEM((2, 8, EDGE), jnp.int32),
            pltpu.VMEM((8, EDGE), jnp.int32),
            pltpu.SMEM((8, EDGE), jnp.int32),
            pltpu.VMEM((8, EDGE), F32),
            pltpu.VMEM((2, 8, EDGE), F32),
            pltpu.VMEM((8, EDGE), F32),
            pltpu.VMEM((visits - 1, 8, EDGE), F32),
            pltpu.VMEM((2, CAP, EDGE, EDGE), BF16),
            pltpu.VMEM((BLOCKS + 2 * CAP, EDGE, EDGE), BF16),
            pltpu.VMEM((SLOT_COLS, EXT_ROWS, EDGE), F32),
            pltpu.VMEM((2, SLOT_COLS, HALO, EDGE), BF16),
            pltpu.VMEM((2, SLOT_COLS, HALO, EDGE), BF16),
            pltpu.VMEM((SLOT_COLS + 2, EXT_PAIRS, SEGS, 2 * EDGE), BF16),
            pltpu.VMEM((EXT_PAIRS + 2, SEGS, 2 * EDGE), BF16),
            pltpu.VMEM((2, SLOT_COLS, EXT_PAIRS, SEGS, EDGE), BF16),
            pltpu.VMEM((4 * EDGE, 2 * EDGE), BF16),
            pltpu.VMEM((DEPTH, 2 * EDGE), BF16),
            pltpu.VMEM((ROWS, EDGE), F32),
            pltpu.VMEM((chips, ROWS, EDGE), BF16),
            pltpu.VMEM((chips, ROWS, EDGE), BF16),
            pltpu.VMEM((chips - 1, 2, HALF_ROWS, EDGE), BF16),
            pltpu.VMEM((chips - 1, 2, HALF_ROWS, EDGE), BF16),
            dma((10,)),
            dma((2, CAP // CHUNK)),
            dma((2, CAP // CHUNK)),
            dma((2, 2)),
            dma((2, 2)),
            dma((2,)),
            dma((2,)),
            dma((chips,)),
            dma((chips,)),
            dma((chips - 1, 2)),
            dma((chips - 1, 2)),
            dma((visits - 1,)),
            dma((visits - 1,)),
        ],
        compiler_params=pltpu.CompilerParams(
            collective_id=0, has_side_effects=True, vmem_limit_bytes=56 << 20
        ),
        name="coadd",
    )(send_list, block_slot, block_offset, block_frac, inv_var, psf, blocks)


def on_device(blocks, send_list, block_slot, block_offset, block_frac, inv_var, psf_kernel):
    return coadd(
        send_list[0, 0],
        block_slot,
        block_offset[0].T,
        block_frac[0].T,
        inv_var,
        jnp.transpose(psf_kernel, (1, 0, 2)),
        blocks[0],
    )


def solution(mesh):
    in_specs = (
        P("visit", "patch", None, None),
        P("visit", "patch", None, None),
        P("visit", "patch"),
        P("visit", "patch", None),
        P("visit", "patch", None),
        P("visit", "patch"),
        P("visit", None, None),
    )
    out_specs = P("patch", "visit")
    return jax.shard_map(
        on_device, mesh=mesh, in_specs=in_specs, out_specs=out_specs, check_vma=False
    )
```

```python
import math

import jax
import jax.numpy as jnp
from jax import lax
from jax.experimental import pallas as pl
from jax.experimental.pallas import tpu as pltpu
from jax.sharding import PartitionSpec as P

EDGE = 128
BLOCKS = 64
CAP = 16
KSIZE = 25
REACH = 12
GROUP = 8
CHUNK = 4
SLOT_COLS = 8
SLOT_ROWS = 8
ROWS = SLOT_ROWS * EDGE
COLS = SLOT_COLS * EDGE
HALO = 16
EXT_ROWS = ROWS + 2 * HALO
SEGS = 16
SEG_ROWS = ROWS // SEGS
PAIRS = SEG_ROWS // 2
STEPS = KSIZE // 2 + 1
EXT_PAIRS = PAIRS + STEPS - 1
SIDE = 2 * REACH
PACK = EDGE // SIDE
HALVES = -(-2 * STEPS // PACK)
DEPTH = STEPS * 2 * EDGE + HALVES * EDGE
HALF_PAIRS = PAIRS // 2
HALF_ROWS = ROWS // 2
LEAD = 3
F32 = jnp.float32
BF16 = jnp.bfloat16


def lanczos_weight(tap_offset):
    inside = jnp.abs(tap_offset) < 3.0
    safe_tap = jnp.where(inside, tap_offset, 1.5)
    value = (
        3.0
        * jnp.sin(math.pi * safe_tap)
        * jnp.sin(math.pi * safe_tap / 3.0)
        / (math.pi * math.pi * safe_tap * safe_tap)
    )
    return jnp.where(inside, value, 0.0)


def column_of(row):
    count = row.shape[1]
    down = lax.broadcasted_iota(jnp.int32, (count, count), 0)
    across = lax.broadcasted_iota(jnp.int32, (count, count), 1)
    spread = jnp.where(down == across, jnp.broadcast_to(row, (count, count)), 0.0)
    return jnp.sum(spread, axis=1, keepdims=True)


def toeplitz(row, rows):
    return pltpu.roll(jnp.broadcast_to(row, (rows, EDGE)), 0, 1, stride=1, stride_axis=0)


def build_taps(psf_ref, psf_rows, taps):
    for a in range(KSIZE):
        psf_rows[a : a + 1, :] = psf_ref[a]
    source = lax.broadcasted_iota(jnp.int32, (KSIZE, EDGE), 0)
    target = lax.broadcasted_iota(jnp.int32, (KSIZE, EDGE), 1)
    flip = jnp.where((target + source) % EDGE == 0, 1.0, 0.0).astype(BF16)
    flipped = jnp.dot(psf_rows[...].astype(BF16), flip, preferred_element_type=F32)
    centred = pltpu.roll(flipped, REACH, 1)
    down = lax.broadcasted_iota(jnp.int32, (EDGE, EDGE), 0)
    across = lax.broadcasted_iota(jnp.int32, (EDGE, EDGE), 1)
    near = jnp.abs(across - down) <= REACH
    beside = (down[:SIDE] < REACH) == (across[:SIDE] < EDGE // 2)

    def lanes(row_out):
        return slice(row_out * EDGE, (row_out + 1) * EDGE)

    for a in range(-1, KSIZE + 1):
        if 0 <= a < KSIZE:
            block = jnp.where(near, toeplitz(centred[a : a + 1], EDGE), 0.0).astype(BF16)
        else:
            block = jnp.zeros((EDGE, EDGE), BF16)
        for row_out in range(2):
            row_in = a + row_out
            if 0 <= row_in < 2 * STEPS:
                taps[row_in * EDGE : (row_in + 1) * EDGE, lanes(row_out)] = block
    for half in range(HALVES):
        for row_out in range(2):
            parts = []
            for i in range(PACK):
                a = PACK * half + i - row_out
                if 0 <= a < KSIZE:
                    parts.append(jnp.where(beside, toeplitz(flipped[a : a + 1], SIDE), 0.0))
                else:
                    parts.append(jnp.zeros((SIDE, EDGE), F32))
            parts.append(jnp.zeros((EDGE - PACK * SIDE, EDGE), F32))
            base = STEPS * 2 * EDGE + half * EDGE
            taps[base : base + EDGE, lanes(row_out)] = jnp.concatenate(parts, axis=0).astype(BF16)


def build_select(select):
    shape = (2 * EDGE, 2 * EDGE)
    source = lax.broadcasted_iota(jnp.int32, shape, 0)
    lane = lax.broadcasted_iota(jnp.int32, shape, 1)
    inner = lax.rem(lane, EDGE)
    q = lax.rem(inner, SIDE)
    wanted = jnp.where(q < REACH, EDGE - REACH + q, q - REACH) + (lane - inner)
    hit = (source == wanted) & (inner < PACK * SIDE)
    select[...] = jnp.where(hit, 1.0, 0.0).astype(BF16)


def remote(src, dst, send_sem, recv_sem, **target):
    return pltpu.make_async_remote_copy(
        src_ref=src,
        dst_ref=dst,
        send_sem=send_sem,
        recv_sem=recv_sem,
        device_id=target,
        device_id_type=pl.DeviceIdType.MESH,
    )


def coadd_kernel(
    list_hbm,
    slot_hbm,
    offset_hbm,
    frac_hbm,
    inv_var_hbm,
    psf_hbm,
    blocks_hbm,
    out_ref,
    lists,
    slots,
    slot_vec,
    offset_vec,
    frac_vec,
    inv_var_vec,
    psf_vec,
    psf_rows,
    raw,
    row_taps,
    col_taps,
    weights,
    staying,
    staying_flat,
    index_mine,
    index_in,
    index_sum,
    index_flat,
    weight_mine,
    weight_in,
    weight_sum,
    weight_all,
    outgoing,
    held,
    wide,
    halo_out,
    halo_in,
    centre,
    edges,
    fresh,
    sides,
    select,
    taps,
    own_part,
    pair_out,
    pair_in,
    chip_out,
    chip_in,
    local_sem,
    block_send,
    block_recv,
    meta_send,
    meta_recv,
    halo_send,
    halo_recv,
    pair_send,
    pair_recv,
    chip_send,
    chip_recv,
    weight_send,
    weight_recv,
):
    patch = lax.axis_index("patch")
    last = lax.axis_size("patch") - 1
    visit = lax.axis_index("visit")
    visits = lax.axis_size("visit")
    chips = visits // 2
    chip, core = visit // 2, lax.rem(visit, 2)
    partner = visit + 1 - 2 * core
    has_low, has_high = patch > 0, patch < last
    sides_of = (
        (has_low, jnp.maximum(patch - 1, 0)),
        (has_high, jnp.minimum(patch + 1, last)),
    )

    loads = [
        pltpu.make_async_copy(src, dst, local_sem.at[i])
        for i, (src, dst) in enumerate(
            (
                (offset_hbm, offset_vec),
                (frac_hbm, frac_vec),
                (inv_var_hbm, inv_var_vec),
                (list_hbm, lists),
                (slot_hbm, slots),
                (slot_hbm, slot_vec),
                (psf_hbm, psf_vec),
                (blocks_hbm, raw),
            )
        )
    ]
    for load in loads:
        load.start()

    barrier = pltpu.get_barrier_semaphore()
    for there, neighbour in sides_of:

        @pl.when(there)
        def greet():
            pl.semaphore_signal(
                barrier, inc=1, device_id={"patch": neighbour}, device_id_type=pl.DeviceIdType.MESH
            )

    for d in range(1, visits):
        pl.semaphore_signal(
            barrier,
            inc=1,
            device_id={"visit": lax.rem(visit + d, visits)},
            device_id_type=pl.DeviceIdType.MESH,
        )

    for load in loads[:3]:
        load.wait()
    shift_rows = column_of(offset_vec[0:1, :].astype(F32) + frac_vec[0:1, :].astype(F32))
    shift_cols = column_of(offset_vec[1:2, :].astype(F32) + frac_vec[1:2, :].astype(F32))
    lane_block = lax.broadcasted_iota(jnp.int32, (BLOCKS, EDGE), 1)
    signed = jnp.where(lane_block < EDGE // 2, lane_block, lane_block - EDGE).astype(F32)
    row_taps[...] = lanczos_weight(signed - shift_rows).astype(BF16).astype(F32)
    col_taps[...] = lanczos_weight(-signed - shift_cols).astype(BF16).astype(F32)
    weights[...] = jnp.broadcast_to(column_of(inv_var_vec[...].astype(F32)), (BLOCKS, EDGE))

    down = lax.broadcasted_iota(jnp.int32, (EDGE, EDGE), 0)
    across = lax.broadcasted_iota(jnp.int32, (EDGE, EDGE), 1)
    near = jnp.abs(down - across) < EDGE // 2

    def band(taps_ref, j):
        rolled = toeplitz(taps_ref[pl.ds(j, 1), :], EDGE)
        return jnp.where(near, rolled, 0.0).astype(BF16)

    def warped(j):
        first = jnp.dot(band(row_taps, j), raw[j], preferred_element_type=F32)
        second = jnp.dot(first.astype(BF16), band(col_taps, j), preferred_element_type=F32)
        return (second.astype(BF16).astype(F32) * weights[pl.ds(j, 1), :]).astype(BF16)

    def block_copy(side, chunk, neighbour):
        lands = 1 - side
        return remote(
            outgoing.at[side, pl.ds(chunk * CHUNK, CHUNK)],
            held.at[pl.ds(BLOCKS + lands * CAP + chunk * CHUNK, CHUNK)],
            block_send.at[side, chunk],
            block_recv.at[lands, chunk],
            patch=neighbour,
        )

    def meta_copy(side, kind, neighbour):
        lands = 1 - side
        src, dst = ((index_mine, index_in), (weight_mine, weight_in))[kind]
        return remote(
            src, dst.at[lands], meta_send.at[side, kind], meta_recv.at[lands, kind], patch=neighbour
        )

    def halo_copy(side, neighbour):
        lands = 1 - side
        return remote(
            halo_out.at[side], halo_in.at[lands], halo_send.at[side], halo_recv.at[lands], patch=neighbour
        )

    for load in loads[3:]:
        load.wait()
    pl.semaphore_wait(barrier, visits - 1 + has_low.astype(jnp.int32) + has_high.astype(jnp.int32))

    def leave(chunk, carry):
        for side in range(2):
            for i in range(CHUNK):
                t = chunk * CHUNK + i
                outgoing[side, t] = warped(jnp.maximum(lists[side, t], 0))
        for side, (there, neighbour) in enumerate(sides_of):

            @pl.when(there)
            def send():
                block_copy(side, chunk, neighbour).start()

        return carry

    lax.fori_loop(0, CAP // CHUNK, leave, 0)

    lane = lax.broadcasted_iota(jnp.int32, (1, EDGE), 1)

    def list_leaving(t, carry):
        leaving, index_low, index_high, weight_low, weight_high = carry
        found = []
        for side in range(2):
            j = lists[side, t]
            inside = jnp.maximum(j, 0)
            leaving = jnp.where(lane == j, 1, leaving)
            here = (lane == slots[0, inside]) & (jnp.broadcast_to(j, (1, EDGE)) >= 0)
            code = BLOCKS + (1 - side) * CAP + t + 1
            found.append((jnp.where(here, code, 0), jnp.where(here, weights[pl.ds(inside, 1), :], 0.0)))
        return (
            leaving,
            index_low + found[0][0],
            index_high + found[1][0],
            weight_low + found[0][1],
            weight_high + found[1][1],
        )

    zeros_i = jnp.zeros((1, EDGE), jnp.int32)
    zeros_f = jnp.zeros((1, EDGE), F32)
    leaving, index_low, index_high, weight_low, weight_high = lax.fori_loop(
        0, CAP, list_leaving, (zeros_i, zeros_i, zeros_i, zeros_f, zeros_f)
    )
    staying[...] = jnp.full((8, EDGE), EDGE, jnp.int32)
    staying[0:1, 0:BLOCKS] = jnp.where(leaving[:, 0:BLOCKS] > 0, EDGE, slot_vec[...])
    flat = pltpu.make_async_copy(staying, staying_flat, local_sem.at[8])
    flat.start()
    flat.wait()

    def list_staying(j, carry):
        index_own, weight_own = carry
        here = lane == staying_flat[0, j]
        return (
            index_own + jnp.where(here, j + 1, 0),
            weight_own + jnp.where(here, weights[pl.ds(j, 1), :], 0.0),
        )

    index_own, weight_own = lax.fori_loop(0, BLOCKS, list_staying, (zeros_i, zeros_f))
    index_mine[...] = jnp.zeros((8, EDGE), jnp.int32)
    weight_mine[...] = jnp.zeros((8, EDGE), F32)
    for k, (index, weight) in enumerate(
        ((index_own, weight_own), (index_low, weight_low), (index_high, weight_high))
    ):
        index_mine[k : k + 1, :] = index
        weight_mine[k : k + 1, :] = weight
    for side, (there, neighbour) in enumerate(sides_of):

        @pl.when(there)
        def send_meta():
            for kind in range(2):
                meta_copy(side, kind, neighbour).start()

        @pl.when(jnp.logical_not(there))
        def nothing_comes():
            index_in[side] = jnp.zeros((8, EDGE), jnp.int32)
            weight_in[side] = jnp.zeros((8, EDGE), F32)
            halo_in[side] = jnp.zeros((SLOT_COLS, HALO, EDGE), BF16)

    def warp_group(group, carry):
        for i in range(GROUP):
            j = group * GROUP + i
            held[j] = warped(j)
        return carry

    lax.fori_loop(0, BLOCKS // GROUP, warp_group, 0)

    build_taps(psf_vec, psf_rows, taps)
    build_select(select)
    blank = jnp.zeros((EXT_PAIRS, SEGS, 2 * EDGE), BF16)
    centre[0] = blank
    centre[SLOT_COLS + 1] = blank
    edges[EXT_PAIRS : EXT_PAIRS + 2] = jnp.zeros((2, SEGS, 2 * EDGE), BF16)

    for side, (there, neighbour) in enumerate(sides_of):

        @pl.when(there)
        def meta_arrives():
            for kind in range(2):
                meta_copy(1 - side, kind, neighbour).wait_recv()

    index_sum[...] = jnp.zeros((8, EDGE), jnp.int32)
    found = index_mine[0:1, :] + index_in[0, 2:3, :] + index_in[1, 1:2, :]
    index_sum[0:1, :] = jnp.clip(found, 1, BLOCKS + 2 * CAP) - 1
    weight_sum[...] = jnp.zeros((8, EDGE), F32)
    weight_sum[0:1, :] = weight_mine[0:1, :] + weight_in[0, 2:3, :] + weight_in[1, 1:2, :]

    def weight_copy(d):
        return remote(
            weight_sum,
            weight_all.at[d - 1],
            weight_send.at[d - 1],
            weight_recv.at[d - 1],
            visit=lax.rem(visit + d, visits),
        )

    for d in range(1, visits):
        weight_copy(d).start()
    flat = pltpu.make_async_copy(index_sum, index_flat, local_sem.at[9])
    flat.start()
    flat.wait()
    for side, (there, neighbour) in enumerate(sides_of):

        @pl.when(there)
        def blocks_arrive():
            for chunk in range(CAP // CHUNK):
                block_copy(1 - side, chunk, neighbour).wait_recv()

    def put(slot_row, carry):
        for slot_col in range(SLOT_COLS):
            source = index_flat[0, slot_row * SLOT_COLS + slot_col]
            top = pl.multiple_of(HALO + slot_row * EDGE, HALO)
            wide[slot_col, pl.ds(top, EDGE), :] = held[source].astype(F32)
        return carry

    lax.fori_loop(0, 2, lambda i, carry: put(i * (SLOT_ROWS - 1), carry), 0)
    halo_out[0] = wide[:, HALO : 2 * HALO, :].astype(BF16)
    halo_out[1] = wide[:, ROWS : ROWS + HALO, :].astype(BF16)
    for side, (there, neighbour) in enumerate(sides_of):

        @pl.when(there)
        def send_halo():
            halo_copy(side, neighbour).start()

    lax.fori_loop(1, SLOT_ROWS - 1, put, 0)

    def to_pairs(g, carry):
        for row_in in range(2):
            start = 2 * g + (HALO - REACH) + row_in
            for w in range(SLOT_COLS):
                rows = wide[w, pl.ds(start, SEGS, stride=SEG_ROWS), :]
                centre[w + 1, g, :, row_in * EDGE : (row_in + 1) * EDGE] = rows.astype(BF16)
        return carry

    lax.fori_loop(REACH // 2, REACH // 2 + PAIRS, to_pairs, 0)
    for side, (there, neighbour) in enumerate(sides_of):

        @pl.when(there)
        def halo_arrives():
            halo_copy(1 - side, neighbour).wait_recv()

    wide[:, 0:HALO, :] = halo_in[0].astype(F32)
    wide[:, HALO + ROWS : EXT_ROWS, :] = halo_in[1].astype(F32)
    lax.fori_loop(0, REACH // 2, to_pairs, 0)
    lax.fori_loop(REACH // 2 + PAIRS, EXT_PAIRS, to_pairs, 0)

    lane_seg = lax.broadcasted_iota(jnp.int32, (SEGS, EDGE), 1)

    lane_pack = lane_seg.astype(BF16)
    lane_all = lax.broadcasted_iota(jnp.int32, (EXT_PAIRS * SEGS, EDGE), 1).astype(BF16)
    from_right = lane_all < EDGE // 2

    def place_edges(w):
        left, right = (centre[w + k].reshape(EXT_PAIRS * SEGS, 2 * EDGE) for k in (0, 2))
        both = jnp.concatenate(
            [
                jnp.where(from_right, right[:, n * EDGE : (n + 1) * EDGE], left[:, n * EDGE : (n + 1) * EDGE])
                for n in range(2)
            ],
            axis=1,
        )
        placed = jnp.dot(both, select[...], preferred_element_type=F32)
        edges[0:EXT_PAIRS] = placed.astype(BF16).reshape(EXT_PAIRS, SEGS, 2 * EDGE)

    def pack_edges():
        for g in range(EXT_PAIRS):
            rows = [edges[g + n // 2, :, (n % 2) * EDGE : (n % 2 + 1) * EDGE] for n in range(PACK + 1)]
            for odd in range(2):
                packed = rows[odd + PACK - 1]
                for n in range(PACK - 2, -1, -1):
                    packed = jnp.where(lane_pack < (n + 1) * SIDE, rows[odd + n], packed)
                fresh[odd, g] = packed

    def tile_at(turn):
        distance = jnp.where(turn < 2, 2, jnp.where(turn < 6, 1 + 2 * lax.rem(turn, 2), 0))
        is_mine = (turn == 1) | (turn == 4) | (turn == 5) | (turn == 7)
        return 2 * lax.rem(chip + distance, chips) + jnp.where(is_mine, core, 1 - core)

    def first_sides(turn, carry):
        w = tile_at(turn)
        place_edges(w)
        pack_edges()
        sides[:, w] = fresh[...]
        return carry

    lax.fori_loop(0, LEAD, first_sides, 0)

    def pair_copy(k):
        return remote(pair_out.at[k], pair_in.at[k], pair_send.at[k], pair_recv.at[k], visit=partner)

    ways = (
        2 * lax.rem(chip + 1, chips) + core,
        2 * lax.rem(chip + chips - 1, chips) + core,
    )

    def chip_copy(k, way):
        return remote(
            chip_out.at[k, way],
            chip_in.at[k, way],
            chip_send.at[k, way],
            chip_recv.at[k, way],
            visit=ways[way],
        )

    def half_tile(w, half):
        first = half * HALF_PAIRS
        columns = [
            centre[w + 1, pl.ds(first + t, HALF_PAIRS)].reshape(HALF_ROWS // 2, 2 * EDGE) for t in range(STEPS)
        ]
        for part in range(HALVES):
            row = PACK * part
            columns.append(
                sides[row % 2, w, pl.ds(first + row // 2, HALF_PAIRS)].reshape(HALF_ROWS // 2, EDGE)
            )
        return columns

    strip = 2 * EDGE

    def tile_step(i, carry):
        k = i // 2
        mine = lax.rem(i, 2)
        to_core = jnp.where(mine == 1, core, 1 - core)
        ahead = jnp.where(k == 0, 2, jnp.where(k == chips - 1, 0, 1))
        behind = jnp.where(k == 0, 2, jnp.where(k == chips - 1, 0, chips - 1))
        half = jnp.where(k == 1, 1, 0)
        upper = half_tile(2 * lax.rem(chip + ahead, chips) + to_core, half)
        lower = half_tile(2 * lax.rem(chip + behind, chips) + to_core, 1 - half)
        both = jnp.concatenate(
            [jnp.concatenate([a, b], axis=0) for a, b in zip(upper, lower)], axis=1
        )
        coming = tile_at(jnp.minimum(i + LEAD, SLOT_COLS - 1))
        place_edges(coming)
        acc = jnp.dot(both, taps[...], preferred_element_type=F32)
        pack_edges()

        def pieces():
            for way in range(2):
                for row_out in range(2):
                    first = way * HALF_ROWS + row_out * (HALF_ROWS // 2)
                    yield slice(first, first + HALF_ROWS // 2), acc[
                        way * (HALF_ROWS // 2) : (way + 1) * (HALF_ROWS // 2),
                        row_out * EDGE : (row_out + 1) * EDGE,
                    ]

        sides[:, coming] = fresh[...]

        @pl.when(mine == 0)
        def for_partner():
            for rows, value in pieces():
                pair_out[k, rows, :] = value.astype(BF16)
            pair_copy(k).start()

        @pl.when(mine == 1)
        def for_this_core():
            for rows, value in pieces():
                own_part[rows, :] = value
            pair_copy(k).wait_recv()

            def send(extra):
                for way in range(2):
                    if extra:
                        chip_copy(0, way).wait_recv()

                    def add(r, inner):
                        here = pl.ds(pl.multiple_of(r * strip, strip), strip)
                        rows = pl.ds(pl.multiple_of(way * HALF_ROWS + r * strip, strip), strip)
                        value = own_part[rows, :] + pair_in[k, rows, :].astype(F32)
                        if extra:
                            value = value + chip_in[0, way, here, :].astype(F32)
                        chip_out[k, way, here, :] = value.astype(BF16)
                        return inner

                    lax.fori_loop(0, HALF_ROWS // strip, add, 0)
                    chip_copy(k, way).start()

            @pl.when(k < 2)
            def plain():
                send(False)

            @pl.when(k == 2)
            def relayed():
                send(True)

        return carry

    lax.fori_loop(0, SLOT_COLS, tile_step, 0)

    for d in range(1, visits):
        weight_copy(d).wait_recv()
    denom = weight_sum[0:1, :]
    for d in range(1, visits):
        denom = denom + weight_all[d - 1, 0:1, :]
    row_seg = lax.broadcasted_iota(jnp.int32, (SEGS, EDGE), 0)
    wanted = (row_seg // 2) * SLOT_COLS + visit
    denom = jnp.sum(
        jnp.where(lane_seg == wanted, jnp.broadcast_to(denom, (SEGS, EDGE)), 0.0), axis=1, keepdims=True
    )
    denom = jnp.broadcast_to(denom, (SEGS, EDGE))
    for k in (1, 2):
        for way in range(2):
            chip_copy(k, way).wait_recv()

    def finish(g, carry):
        for half in range(2):
            for row_out in range(2):
                base = row_out * (HALF_ROWS // 2) + g * SEGS
                here = pl.ds(pl.multiple_of(base, SEGS), SEGS)
                rows = pl.ds(pl.multiple_of(half * HALF_ROWS + base, SEGS), SEGS)
                value = own_part[rows, :] + pair_in[chips - 1, rows, :].astype(F32)
                value = value + chip_in[1, 1 - half, here, :].astype(F32)
                value = value + chip_in[2, half, here, :].astype(F32)
                start = 2 * (half * HALF_PAIRS + g) + row_out
                out_ref[pl.ds(start, SEGS, stride=SEG_ROWS), :] = value / denom
        return carry

    lax.fori_loop(0, HALF_PAIRS, finish, 0)

    for side, (there, neighbour) in enumerate(sides_of):

        @pl.when(there)
        def sent():
            for chunk in range(CAP // CHUNK):
                block_copy(side, chunk, neighbour).wait_send()
            for kind in range(2):
                meta_copy(side, kind, neighbour).wait_send()
            halo_copy(side, neighbour).wait_send()

    for k in range(chips):
        pair_copy(k).wait_send()
    for k in range(chips - 1):
        for way in range(2):
            chip_copy(k, way).wait_send()
    for d in range(1, visits):
        weight_copy(d).wait_send()


def coadd(send_list, block_slot, block_offset, block_frac, inv_var, psf, blocks):
    visits = lax.axis_size("visit")
    chips = visits // 2
    hbm = pl.BlockSpec(memory_space=pl.ANY)
    dma = pltpu.SemaphoreType.DMA
    return pl.pallas_call(
        coadd_kernel,
        out_shape=jax.ShapeDtypeStruct((ROWS, EDGE), F32),
        in_specs=[hbm] * 7,
        out_specs=pl.BlockSpec(memory_space=pltpu.VMEM),
        scratch_shapes=[
            pltpu.SMEM((2, CAP), jnp.int32),
            pltpu.SMEM((1, BLOCKS), jnp.int32),
            pltpu.VMEM((1, BLOCKS), jnp.int32),
            pltpu.VMEM((2, BLOCKS), jnp.int32),
            pltpu.VMEM((2, BLOCKS), BF16),
            pltpu.VMEM((1, BLOCKS), BF16),
            pltpu.VMEM((KSIZE, 1, KSIZE), F32),
            pltpu.VMEM((KSIZE, KSIZE), F32),
            pltpu.VMEM((BLOCKS, EDGE, EDGE), BF16),
            pltpu.VMEM((BLOCKS, EDGE), F32),
            pltpu.VMEM((BLOCKS, EDGE), F32),
            pltpu.VMEM((BLOCKS, EDGE), F32),
            pltpu.VMEM((8, EDGE), jnp.int32),
            pltpu.SMEM((8, EDGE), jnp.int32),
            pltpu.VMEM((8, EDGE), jnp.int32),
            pltpu.VMEM((2, 8, EDGE), jnp.int32),
            pltpu.VMEM((8, EDGE), jnp.int32),
            pltpu.SMEM((8, EDGE), jnp.int32),
            pltpu.VMEM((8, EDGE), F32),
            pltpu.VMEM((2, 8, EDGE), F32),
            pltpu.VMEM((8, EDGE), F32),
            pltpu.VMEM((visits - 1, 8, EDGE), F32),
            pltpu.VMEM((2, CAP, EDGE, EDGE), BF16),
            pltpu.VMEM((BLOCKS + 2 * CAP, EDGE, EDGE), BF16),
            pltpu.VMEM((SLOT_COLS, EXT_ROWS, EDGE), F32),
            pltpu.VMEM((2, SLOT_COLS, HALO, EDGE), BF16),
            pltpu.VMEM((2, SLOT_COLS, HALO, EDGE), BF16),
            pltpu.VMEM((SLOT_COLS + 2, EXT_PAIRS, SEGS, 2 * EDGE), BF16),
            pltpu.VMEM((EXT_PAIRS + 2, SEGS, 2 * EDGE), BF16),
            pltpu.VMEM((2, EXT_PAIRS, SEGS, EDGE), BF16),
            pltpu.VMEM((2, SLOT_COLS, EXT_PAIRS, SEGS, EDGE), BF16),
            pltpu.VMEM((2 * EDGE, 2 * EDGE), BF16),
            pltpu.VMEM((DEPTH, 2 * EDGE), BF16),
            pltpu.VMEM((ROWS, EDGE), F32),
            pltpu.VMEM((chips, ROWS, EDGE), BF16),
            pltpu.VMEM((chips, ROWS, EDGE), BF16),
            pltpu.VMEM((chips - 1, 2, HALF_ROWS, EDGE), BF16),
            pltpu.VMEM((chips - 1, 2, HALF_ROWS, EDGE), BF16),
            dma((10,)),
            dma((2, CAP // CHUNK)),
            dma((2, CAP // CHUNK)),
            dma((2, 2)),
            dma((2, 2)),
            dma((2,)),
            dma((2,)),
            dma((chips,)),
            dma((chips,)),
            dma((chips - 1, 2)),
            dma((chips - 1, 2)),
            dma((visits - 1,)),
            dma((visits - 1,)),
        ],
        compiler_params=pltpu.CompilerParams(
            collective_id=0, has_side_effects=True, vmem_limit_bytes=56 << 20
        ),
        name="coadd",
    )(send_list, block_slot, block_offset, block_frac, inv_var, psf, blocks)


def on_device(blocks, send_list, block_slot, block_offset, block_frac, inv_var, psf_kernel):
    return coadd(
        send_list[0, 0],
        block_slot,
        block_offset[0].T,
        block_frac[0].T,
        inv_var,
        jnp.transpose(psf_kernel, (1, 0, 2)),
        blocks[0],
    )


def solution(mesh):
    in_specs = (
        P("visit", "patch", None, None),
        P("visit", "patch", None, None),
        P("visit", "patch"),
        P("visit", "patch", None),
        P("visit", "patch", None),
        P("visit", "patch"),
        P("visit", None, None),
    )
    out_specs = P("patch", "visit")
    return jax.shard_map(
        on_device, mesh=mesh, in_specs=in_specs, out_specs=out_specs, check_vma=False
    )
```

```python
import math

import jax
import jax.numpy as jnp
from jax import lax
from jax.experimental import pallas as pl
from jax.experimental.pallas import tpu as pltpu
from jax.sharding import PartitionSpec as P

EDGE = 128
BLOCKS = 64
CAP = 16
KSIZE = 25
REACH = 12
GROUP = 8
CHUNK = 4
SLOT_COLS = 8
SLOT_ROWS = 8
ROWS = SLOT_ROWS * EDGE
COLS = SLOT_COLS * EDGE
HALO = 16
EXT_ROWS = ROWS + 2 * HALO
SEGS = 16
SEG_ROWS = ROWS // SEGS
PAIRS = SEG_ROWS // 2
STEPS = KSIZE // 2 + 1
EXT_PAIRS = PAIRS + STEPS - 1
SIDE = 2 * REACH
PACK = EDGE // SIDE
HALVES = -(-2 * STEPS // PACK)
DEPTH = STEPS * 2 * EDGE + HALVES * EDGE
HALF_PAIRS = PAIRS // 2
HALF_ROWS = ROWS // 2
LEAD = 3
F32 = jnp.float32
BF16 = jnp.bfloat16


def lanczos_weight(tap_offset):
    inside = jnp.abs(tap_offset) < 3.0
    safe_tap = jnp.where(inside, tap_offset, 1.5)
    value = (
        3.0
        * jnp.sin(math.pi * safe_tap)
        * jnp.sin(math.pi * safe_tap / 3.0)
        / (math.pi * math.pi * safe_tap * safe_tap)
    )
    return jnp.where(inside, value, 0.0)


def column_of(row):
    count = row.shape[1]
    down = lax.broadcasted_iota(jnp.int32, (count, count), 0)
    across = lax.broadcasted_iota(jnp.int32, (count, count), 1)
    spread = jnp.where(down == across, jnp.broadcast_to(row, (count, count)), 0.0)
    return jnp.sum(spread, axis=1, keepdims=True)


def toeplitz(row, rows):
    return pltpu.roll(jnp.broadcast_to(row, (rows, EDGE)), 0, 1, stride=1, stride_axis=0)


def build_taps(psf_ref, psf_rows, taps):
    for a in range(KSIZE):
        psf_rows[a : a + 1, :] = psf_ref[a]
    source = lax.broadcasted_iota(jnp.int32, (KSIZE, EDGE), 0)
    target = lax.broadcasted_iota(jnp.int32, (KSIZE, EDGE), 1)
    flip = jnp.where((target + source) % EDGE == 0, 1.0, 0.0).astype(BF16)
    flipped = jnp.dot(psf_rows[...].astype(BF16), flip, preferred_element_type=F32)
    centred = pltpu.roll(flipped, REACH, 1)
    down = lax.broadcasted_iota(jnp.int32, (EDGE, EDGE), 0)
    across = lax.broadcasted_iota(jnp.int32, (EDGE, EDGE), 1)
    near = jnp.abs(across - down) <= REACH
    beside = (down[:SIDE] < REACH) == (across[:SIDE] < EDGE // 2)

    def lanes(row_out):
        return slice(row_out * EDGE, (row_out + 1) * EDGE)

    for a in range(-1, KSIZE + 1):
        if 0 <= a < KSIZE:
            block = jnp.where(near, toeplitz(centred[a : a + 1], EDGE), 0.0).astype(BF16)
        else:
            block = jnp.zeros((EDGE, EDGE), BF16)
        for row_out in range(2):
            row_in = a + row_out
            if 0 <= row_in < 2 * STEPS:
                taps[row_in * EDGE : (row_in + 1) * EDGE, lanes(row_out)] = block
    for half in range(HALVES):
        for row_out in range(2):
            parts = []
            for i in range(PACK):
                a = PACK * half + i - row_out
                if 0 <= a < KSIZE:
                    parts.append(jnp.where(beside, toeplitz(flipped[a : a + 1], SIDE), 0.0))
                else:
                    parts.append(jnp.zeros((SIDE, EDGE), F32))
            parts.append(jnp.zeros((EDGE - PACK * SIDE, EDGE), F32))
            base = STEPS * 2 * EDGE + half * EDGE
            taps[base : base + EDGE, lanes(row_out)] = jnp.concatenate(parts, axis=0).astype(BF16)


def build_select(select):
    shape = (2 * EDGE, 2 * EDGE)
    source = lax.broadcasted_iota(jnp.int32, shape, 0)
    lane = lax.broadcasted_iota(jnp.int32, shape, 1)
    inner = lax.rem(lane, EDGE)
    q = lax.rem(inner, SIDE)
    wanted = jnp.where(q < REACH, EDGE - REACH + q, q - REACH) + (lane - inner)
    hit = (source == wanted) & (inner < PACK * SIDE)
    select[...] = jnp.where(hit, 1.0, 0.0).astype(BF16)


def remote(src, dst, send_sem, recv_sem, **target):
    return pltpu.make_async_remote_copy(
        src_ref=src,
        dst_ref=dst,
        send_sem=send_sem,
        recv_sem=recv_sem,
        device_id=target,
        device_id_type=pl.DeviceIdType.MESH,
    )


def coadd_kernel(
    list_hbm,
    slot_hbm,
    offset_hbm,
    frac_hbm,
    inv_var_hbm,
    psf_hbm,
    blocks_hbm,
    out_ref,
    lists,
    slots,
    slot_vec,
    offset_vec,
    frac_vec,
    inv_var_vec,
    psf_vec,
    psf_rows,
    raw,
    row_taps,
    col_taps,
    weights,
    staying,
    staying_flat,
    index_mine,
    index_in,
    index_sum,
    index_flat,
    weight_mine,
    weight_in,
    weight_sum,
    weight_all,
    outgoing,
    held,
    wide,
    halo_out,
    halo_in,
    centre,
    edges,
    fresh,
    sides,
    select,
    taps,
    own_part,
    pair_out,
    pair_in,
    chip_out,
    chip_in,
    local_sem,
    block_send,
    block_recv,
    meta_send,
    meta_recv,
    halo_send,
    halo_recv,
    pair_send,
    pair_recv,
    chip_send,
    chip_recv,
    weight_send,
    weight_recv,
):
    patch = lax.axis_index("patch")
    last = lax.axis_size("patch") - 1
    visit = lax.axis_index("visit")
    visits = lax.axis_size("visit")
    chips = visits // 2
    chip, core = visit // 2, lax.rem(visit, 2)
    partner = visit + 1 - 2 * core
    has_low, has_high = patch > 0, patch < last
    sides_of = (
        (has_low, jnp.maximum(patch - 1, 0)),
        (has_high, jnp.minimum(patch + 1, last)),
    )

    loads = [
        pltpu.make_async_copy(src, dst, local_sem.at[i])
        for i, (src, dst) in enumerate(
            (
                (offset_hbm, offset_vec),
                (frac_hbm, frac_vec),
                (inv_var_hbm, inv_var_vec),
                (list_hbm, lists),
                (slot_hbm, slots),
                (slot_hbm, slot_vec),
                (psf_hbm, psf_vec),
                (blocks_hbm, raw),
            )
        )
    ]
    for load in loads:
        load.start()

    barrier = pltpu.get_barrier_semaphore()
    for there, neighbour in sides_of:

        @pl.when(there)
        def greet():
            pl.semaphore_signal(
                barrier, inc=1, device_id={"patch": neighbour}, device_id_type=pl.DeviceIdType.MESH
            )

    for d in range(1, visits):
        pl.semaphore_signal(
            barrier,
            inc=1,
            device_id={"visit": lax.rem(visit + d, visits)},
            device_id_type=pl.DeviceIdType.MESH,
        )

    for load in loads[:3]:
        load.wait()
    shift_rows = column_of(offset_vec[0:1, :].astype(F32) + frac_vec[0:1, :].astype(F32))
    shift_cols = column_of(offset_vec[1:2, :].astype(F32) + frac_vec[1:2, :].astype(F32))
    lane_block = lax.broadcasted_iota(jnp.int32, (BLOCKS, EDGE), 1)
    signed = jnp.where(lane_block < EDGE // 2, lane_block, lane_block - EDGE).astype(F32)
    row_taps[...] = lanczos_weight(signed - shift_rows).astype(BF16).astype(F32)
    col_taps[...] = lanczos_weight(-signed - shift_cols).astype(BF16).astype(F32)
    weights[...] = jnp.broadcast_to(column_of(inv_var_vec[...].astype(F32)), (BLOCKS, EDGE))

    down = lax.broadcasted_iota(jnp.int32, (EDGE, EDGE), 0)
    across = lax.broadcasted_iota(jnp.int32, (EDGE, EDGE), 1)
    near = jnp.abs(down - across) < EDGE // 2

    def band(taps_ref, j):
        rolled = toeplitz(taps_ref[pl.ds(j, 1), :], EDGE)
        return jnp.where(near, rolled, 0.0).astype(BF16)

    def warped(j):
        first = jnp.dot(band(row_taps, j), raw[j], preferred_element_type=F32)
        second = jnp.dot(first.astype(BF16), band(col_taps, j), preferred_element_type=F32)
        return (second.astype(BF16).astype(F32) * weights[pl.ds(j, 1), :]).astype(BF16)

    def block_copy(side, chunk, neighbour):
        lands = 1 - side
        return remote(
            outgoing.at[side, pl.ds(chunk * CHUNK, CHUNK)],
            held.at[pl.ds(BLOCKS + lands * CAP + chunk * CHUNK, CHUNK)],
            block_send.at[side, chunk],
            block_recv.at[lands, chunk],
            patch=neighbour,
        )

    def meta_copy(side, kind, neighbour):
        lands = 1 - side
        src, dst = ((index_mine, index_in), (weight_mine, weight_in))[kind]
        return remote(
            src, dst.at[lands], meta_send.at[side, kind], meta_recv.at[lands, kind], patch=neighbour
        )

    def halo_copy(side, neighbour):
        lands = 1 - side
        return remote(
            halo_out.at[side], halo_in.at[lands], halo_send.at[side], halo_recv.at[lands], patch=neighbour
        )

    for load in loads[3:]:
        load.wait()
    pl.semaphore_wait(barrier, visits - 1 + has_low.astype(jnp.int32) + has_high.astype(jnp.int32))

    def leave(chunk, carry):
        for side in range(2):
            for i in range(CHUNK):
                t = chunk * CHUNK + i
                outgoing[side, t] = warped(jnp.maximum(lists[side, t], 0))
        for side, (there, neighbour) in enumerate(sides_of):

            @pl.when(there)
            def send():
                block_copy(side, chunk, neighbour).start()

        return carry

    lax.fori_loop(0, CAP // CHUNK, leave, 0)

    lane = lax.broadcasted_iota(jnp.int32, (1, EDGE), 1)

    def list_leaving(t, carry):
        leaving, index_low, index_high, weight_low, weight_high = carry
        found = []
        for side in range(2):
            j = lists[side, t]
            inside = jnp.maximum(j, 0)
            leaving = jnp.where(lane == j, 1, leaving)
            here = (lane == slots[0, inside]) & (jnp.broadcast_to(j, (1, EDGE)) >= 0)
            code = BLOCKS + (1 - side) * CAP + t + 1
            found.append((jnp.where(here, code, 0), jnp.where(here, weights[pl.ds(inside, 1), :], 0.0)))
        return (
            leaving,
            index_low + found[0][0],
            index_high + found[1][0],
            weight_low + found[0][1],
            weight_high + found[1][1],
        )

    zeros_i = jnp.zeros((1, EDGE), jnp.int32)
    zeros_f = jnp.zeros((1, EDGE), F32)
    leaving, index_low, index_high, weight_low, weight_high = lax.fori_loop(
        0, CAP, list_leaving, (zeros_i, zeros_i, zeros_i, zeros_f, zeros_f)
    )
    staying[...] = jnp.full((8, EDGE), EDGE, jnp.int32)
    staying[0:1, 0:BLOCKS] = jnp.where(leaving[:, 0:BLOCKS] > 0, EDGE, slot_vec[...])
    flat = pltpu.make_async_copy(staying, staying_flat, local_sem.at[8])
    flat.start()
    flat.wait()

    def list_staying(j, carry):
        index_own, weight_own = carry
        here = lane == staying_flat[0, j]
        return (
            index_own + jnp.where(here, j + 1, 0),
            weight_own + jnp.where(here, weights[pl.ds(j, 1), :], 0.0),
        )

    index_own, weight_own = lax.fori_loop(0, BLOCKS, list_staying, (zeros_i, zeros_f))
    index_mine[...] = jnp.zeros((8, EDGE), jnp.int32)
    weight_mine[...] = jnp.zeros((8, EDGE), F32)
    for k, (index, weight) in enumerate(
        ((index_own, weight_own), (index_low, weight_low), (index_high, weight_high))
    ):
        index_mine[k : k + 1, :] = index
        weight_mine[k : k + 1, :] = weight
    for side, (there, neighbour) in enumerate(sides_of):

        @pl.when(there)
        def send_meta():
            for kind in range(2):
                meta_copy(side, kind, neighbour).start()

        @pl.when(jnp.logical_not(there))
        def nothing_comes():
            index_in[side] = jnp.zeros((8, EDGE), jnp.int32)
            weight_in[side] = jnp.zeros((8, EDGE), F32)
            halo_in[side] = jnp.zeros((SLOT_COLS, HALO, EDGE), BF16)

    def warp_group(group, carry):
        for i in range(GROUP):
            j = group * GROUP + i
            held[j] = warped(j)
        return carry

    lax.fori_loop(0, BLOCKS // GROUP, warp_group, 0)

    build_taps(psf_vec, psf_rows, taps)
    build_select(select)
    blank = jnp.zeros((EXT_PAIRS, SEGS, 2 * EDGE), BF16)
    centre[0] = blank
    centre[SLOT_COLS + 1] = blank
    edges[EXT_PAIRS : EXT_PAIRS + 2] = jnp.zeros((2, SEGS, 2 * EDGE), BF16)

    for side, (there, neighbour) in enumerate(sides_of):

        @pl.when(there)
        def meta_arrives():
            for kind in range(2):
                meta_copy(1 - side, kind, neighbour).wait_recv()

    index_sum[...] = jnp.zeros((8, EDGE), jnp.int32)
    found = index_mine[0:1, :] + index_in[0, 2:3, :] + index_in[1, 1:2, :]
    index_sum[0:1, :] = jnp.clip(found, 1, BLOCKS + 2 * CAP) - 1
    weight_sum[...] = jnp.zeros((8, EDGE), F32)
    weight_sum[0:1, :] = weight_mine[0:1, :] + weight_in[0, 2:3, :] + weight_in[1, 1:2, :]

    def weight_copy(d):
        return remote(
            weight_sum,
            weight_all.at[d - 1],
            weight_send.at[d - 1],
            weight_recv.at[d - 1],
            visit=lax.rem(visit + d, visits),
        )

    for d in range(1, visits):
        weight_copy(d).start()
    flat = pltpu.make_async_copy(index_sum, index_flat, local_sem.at[9])
    flat.start()
    flat.wait()
    for side, (there, neighbour) in enumerate(sides_of):

        @pl.when(there)
        def blocks_arrive():
            for chunk in range(CAP // CHUNK):
                block_copy(1 - side, chunk, neighbour).wait_recv()

    def put(slot_row, carry):
        for slot_col in range(SLOT_COLS):
            source = index_flat[0, slot_row * SLOT_COLS + slot_col]
            top = pl.multiple_of(HALO + slot_row * EDGE, HALO)
            wide[slot_col, pl.ds(top, EDGE), :] = held[source].astype(F32)
        return carry

    lax.fori_loop(0, 2, lambda i, carry: put(i * (SLOT_ROWS - 1), carry), 0)
    halo_out[0] = wide[:, HALO : 2 * HALO, :].astype(BF16)
    halo_out[1] = wide[:, ROWS : ROWS + HALO, :].astype(BF16)
    for side, (there, neighbour) in enumerate(sides_of):

        @pl.when(there)
        def send_halo():
            halo_copy(side, neighbour).start()

    lax.fori_loop(1, SLOT_ROWS - 1, put, 0)

    def to_pairs(g, carry):
        for row_in in range(2):
            start = 2 * g + (HALO - REACH) + row_in
            for w in range(SLOT_COLS):
                rows = wide[w, pl.ds(start, SEGS, stride=SEG_ROWS), :]
                centre[w + 1, g, :, row_in * EDGE : (row_in + 1) * EDGE] = rows.astype(BF16)
        return carry

    lax.fori_loop(REACH // 2, REACH // 2 + PAIRS, to_pairs, 0, unroll=4)
    for side, (there, neighbour) in enumerate(sides_of):

        @pl.when(there)
        def halo_arrives():
            halo_copy(1 - side, neighbour).wait_recv()

    wide[:, 0:HALO, :] = halo_in[0].astype(F32)
    wide[:, HALO + ROWS : EXT_ROWS, :] = halo_in[1].astype(F32)
    lax.fori_loop(0, REACH // 2, to_pairs, 0, unroll=True)
    lax.fori_loop(REACH // 2 + PAIRS, EXT_PAIRS, to_pairs, 0, unroll=True)

    lane_seg = lax.broadcasted_iota(jnp.int32, (SEGS, EDGE), 1)

    lane_pack = lane_seg.astype(BF16)
    lane_all = lax.broadcasted_iota(jnp.int32, (EXT_PAIRS * SEGS, EDGE), 1).astype(BF16)
    from_right = lane_all < EDGE // 2

    def place_edges(w):
        left, right = (centre[w + k].reshape(EXT_PAIRS * SEGS, 2 * EDGE) for k in (0, 2))
        both = jnp.concatenate(
            [
                jnp.where(from_right, right[:, n * EDGE : (n + 1) * EDGE], left[:, n * EDGE : (n + 1) * EDGE])
                for n in range(2)
            ],
            axis=1,
        )
        placed = jnp.dot(both, select[...], preferred_element_type=F32)
        edges[0:EXT_PAIRS] = placed.astype(BF16).reshape(EXT_PAIRS, SEGS, 2 * EDGE)

    def pack_edges():
        for g in range(EXT_PAIRS):
            rows = [edges[g + n // 2, :, (n % 2) * EDGE : (n % 2 + 1) * EDGE] for n in range(PACK + 1)]
            for odd in range(2):
                packed = rows[odd + PACK - 1]
                for n in range(PACK - 2, -1, -1):
                    packed = jnp.where(lane_pack < (n + 1) * SIDE, rows[odd + n], packed)
                fresh[odd, g] = packed

    def tile_at(turn):
        distance = jnp.where(turn < 2, 2, jnp.where(turn < 6, 1 + 2 * lax.rem(turn, 2), 0))
        is_mine = (turn == 1) | (turn == 4) | (turn == 5) | (turn == 7)
        return 2 * lax.rem(chip + distance, chips) + jnp.where(is_mine, core, 1 - core)

    def first_sides(turn, carry):
        w = tile_at(turn)
        place_edges(w)
        pack_edges()
        sides[:, w] = fresh[...]
        return carry

    lax.fori_loop(0, LEAD, first_sides, 0)

    def pair_copy(k):
        return remote(pair_out.at[k], pair_in.at[k], pair_send.at[k], pair_recv.at[k], visit=partner)

    ways = (
        2 * lax.rem(chip + 1, chips) + core,
        2 * lax.rem(chip + chips - 1, chips) + core,
    )

    def chip_copy(k, way):
        return remote(
            chip_out.at[k, way],
            chip_in.at[k, way],
            chip_send.at[k, way],
            chip_recv.at[k, way],
            visit=ways[way],
        )

    def half_tile(w, half):
        first = half * HALF_PAIRS
        columns = [
            centre[w + 1, pl.ds(first + t, HALF_PAIRS)].reshape(HALF_ROWS // 2, 2 * EDGE) for t in range(STEPS)
        ]
        for part in range(HALVES):
            row = PACK * part
            columns.append(
                sides[row % 2, w, pl.ds(first + row // 2, HALF_PAIRS)].reshape(HALF_ROWS // 2, EDGE)
            )
        return columns

    strip = 2 * EDGE

    def tile_step(i, carry):
        k = i // 2
        mine = lax.rem(i, 2)
        to_core = jnp.where(mine == 1, core, 1 - core)
        ahead = jnp.where(k == 0, 2, jnp.where(k == chips - 1, 0, 1))
        behind = jnp.where(k == 0, 2, jnp.where(k == chips - 1, 0, chips - 1))
        half = jnp.where(k == 1, 1, 0)
        upper = half_tile(2 * lax.rem(chip + ahead, chips) + to_core, half)
        lower = half_tile(2 * lax.rem(chip + behind, chips) + to_core, 1 - half)
        both = jnp.concatenate(
            [jnp.concatenate([a, b], axis=0) for a, b in zip(upper, lower)], axis=1
        )
        coming = tile_at(jnp.minimum(i + LEAD, SLOT_COLS - 1))
        place_edges(coming)
        acc = jnp.dot(both, taps[...], preferred_element_type=F32)
        pack_edges()

        def pieces():
            for way in range(2):
                for row_out in range(2):
                    first = way * HALF_ROWS + row_out * (HALF_ROWS // 2)
                    yield slice(first, first + HALF_ROWS // 2), acc[
                        way * (HALF_ROWS // 2) : (way + 1) * (HALF_ROWS // 2),
                        row_out * EDGE : (row_out + 1) * EDGE,
                    ]

        sides[:, coming] = fresh[...]

        @pl.when(mine == 0)
        def for_partner():
            for rows, value in pieces():
                pair_out[k, rows, :] = value.astype(BF16)
            pair_copy(k).start()

        @pl.when(mine == 1)
        def for_this_core():
            for rows, value in pieces():
                own_part[rows, :] = value
            pair_copy(k).wait_recv()

            def send(extra):
                for way in range(2):
                    if extra:
                        chip_copy(0, way).wait_recv()

                    def add(r, inner):
                        here = pl.ds(pl.multiple_of(r * strip, strip), strip)
                        rows = pl.ds(pl.multiple_of(way * HALF_ROWS + r * strip, strip), strip)
                        value = own_part[rows, :] + pair_in[k, rows, :].astype(F32)
                        if extra:
                            value = value + chip_in[0, way, here, :].astype(F32)
                        chip_out[k, way, here, :] = value.astype(BF16)
                        return inner

                    lax.fori_loop(0, HALF_ROWS // strip, add, 0)
                    chip_copy(k, way).start()

            @pl.when(k < 2)
            def plain():
                send(False)

            @pl.when(k == 2)
            def relayed():
                send(True)

        return carry

    lax.fori_loop(0, SLOT_COLS, tile_step, 0)

    for d in range(1, visits):
        weight_copy(d).wait_recv()
    denom = weight_sum[0:1, :]
    for d in range(1, visits):
        denom = denom + weight_all[d - 1, 0:1, :]
    row_seg = lax.broadcasted_iota(jnp.int32, (SEGS, EDGE), 0)
    wanted = (row_seg // 2) * SLOT_COLS + visit
    denom = jnp.sum(
        jnp.where(lane_seg == wanted, jnp.broadcast_to(denom, (SEGS, EDGE)), 0.0), axis=1, keepdims=True
    )
    denom = jnp.broadcast_to(denom, (SEGS, EDGE))
    for k in (1, 2):
        for way in range(2):
            chip_copy(k, way).wait_recv()

    def finish(g, carry):
        for half in range(2):
            for row_out in range(2):
                base = row_out * (HALF_ROWS // 2) + g * SEGS
                here = pl.ds(pl.multiple_of(base, SEGS), SEGS)
                rows = pl.ds(pl.multiple_of(half * HALF_ROWS + base, SEGS), SEGS)
                value = own_part[rows, :] + pair_in[chips - 1, rows, :].astype(F32)
                value = value + chip_in[1, 1 - half, here, :].astype(F32)
                value = value + chip_in[2, half, here, :].astype(F32)
                start = 2 * (half * HALF_PAIRS + g) + row_out
                out_ref[pl.ds(start, SEGS, stride=SEG_ROWS), :] = value / denom
        return carry

    lax.fori_loop(0, HALF_PAIRS, finish, 0)

    for side, (there, neighbour) in enumerate(sides_of):

        @pl.when(there)
        def sent():
            for chunk in range(CAP // CHUNK):
                block_copy(side, chunk, neighbour).wait_send()
            for kind in range(2):
                meta_copy(side, kind, neighbour).wait_send()
            halo_copy(side, neighbour).wait_send()

    for k in range(chips):
        pair_copy(k).wait_send()
    for k in range(chips - 1):
        for way in range(2):
            chip_copy(k, way).wait_send()
    for d in range(1, visits):
        weight_copy(d).wait_send()


def coadd(send_list, block_slot, block_offset, block_frac, inv_var, psf, blocks):
    visits = lax.axis_size("visit")
    chips = visits // 2
    hbm = pl.BlockSpec(memory_space=pl.ANY)
    dma = pltpu.SemaphoreType.DMA
    return pl.pallas_call(
        coadd_kernel,
        out_shape=jax.ShapeDtypeStruct((ROWS, EDGE), F32),
        in_specs=[hbm] * 7,
        out_specs=pl.BlockSpec(memory_space=pltpu.VMEM),
        scratch_shapes=[
            pltpu.SMEM((2, CAP), jnp.int32),
            pltpu.SMEM((1, BLOCKS), jnp.int32),
            pltpu.VMEM((1, BLOCKS), jnp.int32),
            pltpu.VMEM((2, BLOCKS), jnp.int32),
            pltpu.VMEM((2, BLOCKS), BF16),
            pltpu.VMEM((1, BLOCKS), BF16),
            pltpu.VMEM((KSIZE, 1, KSIZE), F32),
            pltpu.VMEM((KSIZE, KSIZE), F32),
            pltpu.VMEM((BLOCKS, EDGE, EDGE), BF16),
            pltpu.VMEM((BLOCKS, EDGE), F32),
            pltpu.VMEM((BLOCKS, EDGE), F32),
            pltpu.VMEM((BLOCKS, EDGE), F32),
            pltpu.VMEM((8, EDGE), jnp.int32),
            pltpu.SMEM((8, EDGE), jnp.int32),
            pltpu.VMEM((8, EDGE), jnp.int32),
            pltpu.VMEM((2, 8, EDGE), jnp.int32),
            pltpu.VMEM((8, EDGE), jnp.int32),
            pltpu.SMEM((8, EDGE), jnp.int32),
            pltpu.VMEM((8, EDGE), F32),
            pltpu.VMEM((2, 8, EDGE), F32),
            pltpu.VMEM((8, EDGE), F32),
            pltpu.VMEM((visits - 1, 8, EDGE), F32),
            pltpu.VMEM((2, CAP, EDGE, EDGE), BF16),
            pltpu.VMEM((BLOCKS + 2 * CAP, EDGE, EDGE), BF16),
            pltpu.VMEM((SLOT_COLS, EXT_ROWS, EDGE), F32),
            pltpu.VMEM((2, SLOT_COLS, HALO, EDGE), BF16),
            pltpu.VMEM((2, SLOT_COLS, HALO, EDGE), BF16),
            pltpu.VMEM((SLOT_COLS + 2, EXT_PAIRS, SEGS, 2 * EDGE), BF16),
            pltpu.VMEM((EXT_PAIRS + 2, SEGS, 2 * EDGE), BF16),
            pltpu.VMEM((2, EXT_PAIRS, SEGS, EDGE), BF16),
            pltpu.VMEM((2, SLOT_COLS, EXT_PAIRS, SEGS, EDGE), BF16),
            pltpu.VMEM((2 * EDGE, 2 * EDGE), BF16),
            pltpu.VMEM((DEPTH, 2 * EDGE), BF16),
            pltpu.VMEM((ROWS, EDGE), F32),
            pltpu.VMEM((chips, ROWS, EDGE), BF16),
            pltpu.VMEM((chips, ROWS, EDGE), BF16),
            pltpu.VMEM((chips - 1, 2, HALF_ROWS, EDGE), BF16),
            pltpu.VMEM((chips - 1, 2, HALF_ROWS, EDGE), BF16),
            dma((10,)),
            dma((2, CAP // CHUNK)),
            dma((2, CAP // CHUNK)),
            dma((2, 2)),
            dma((2, 2)),
            dma((2,)),
            dma((2,)),
            dma((chips,)),
            dma((chips,)),
            dma((chips - 1, 2)),
            dma((chips - 1, 2)),
            dma((visits - 1,)),
            dma((visits - 1,)),
        ],
        compiler_params=pltpu.CompilerParams(
            collective_id=0, has_side_effects=True, vmem_limit_bytes=56 << 20
        ),
        name="coadd",
    )(send_list, block_slot, block_offset, block_frac, inv_var, psf, blocks)


def on_device(blocks, send_list, block_slot, block_offset, block_frac, inv_var, psf_kernel):
    return coadd(
        send_list[0, 0],
        block_slot,
        block_offset[0].T,
        block_frac[0].T,
        inv_var,
        jnp.transpose(psf_kernel, (1, 0, 2)),
        blocks[0],
    )


def solution(mesh):
    in_specs = (
        P("visit", "patch", None, None),
        P("visit", "patch", None, None),
        P("visit", "patch"),
        P("visit", "patch", None),
        P("visit", "patch", None),
        P("visit", "patch"),
        P("visit", None, None),
    )
    out_specs = P("patch", "visit")
    return jax.shard_map(
        on_device, mesh=mesh, in_specs=in_specs, out_specs=out_specs, check_vma=False
    )
```
